512 devices in a mesh: nodes: 128 (over z, x, core), mp: 4 (over y).
Axes of the slice: x: 4, y: 4, z: 16, core: 2. Of those that a mesh axis runs over, the one named last changes fastest.
Arguments:
- features: bfloat16 [16384, 1024], P('nodes'), may hold values from -24 to 24
- qkv_weight: bfloat16 [1024, 3, 1024], P(None, None, 'mp'), may hold values from -0.5 to 0.5
- vnode_emb: bfloat16 [4, 1024], replicated, may hold values from -6 to 6
- edge_bias: float32 [3, 8], P(None, 'mp'), may hold values from -1 to 1
- out_grad: bfloat16 [16384, 1024], P('nodes', 'mp'), may hold values from -6 to 6
- neighbours: int32 [4, 16384], P(None, 'nodes'), may hold values from 0 to 16383, as said below
- member: int32 [16384, 4], P('nodes'), may hold values 0 or 1
- tile_list: int32 [128, 3, 2], P('nodes'), may hold values from 0 to 2, as said below
- tile_count: int32 [128], P('nodes'), may hold values from 3 to 3
Outputs:
- feature_grad: bfloat16 [16384, 1024], P('nodes', 'mp')
- weight_grad: float32 [1024, 3, 1024], P('nodes', None, 'mp')
- vnode_grad: float32 [4, 1024], replicated
The draws below stay inside these ranges and needn't reach their ends.
Inputs may be any that keep to these rules, and one draw needn't show every extreme that they name: `neighbours`: each row is a permutation of the 16384 nodes; for each row, exactly 1 of one shard's nodes have their neighbour on any one given shard. `tile_list`: for every shard the 3 entries list each pair (query block below 1, extended key block below 3) once: the 1 pairs (q, q + 1) of a query block q first, then (0, 0) and (0, 2).
All inputs are finite; a program needn't handle non-finite values. No bound on the sum of `member` on one device may be relied on, other than what follows from the above.
Results may differ from the reference program's by a relative error of at most 0.014.
Values may be sent and summed in bfloat16 or wider, within the bound.
No kernel may reach another device: no remote copies, remote signals or barrier semaphores. Data moves between devices by JAX's collectives and lax.ppermute only.
A program may use at most 64 MiB of HBM per device.

```python
import math
import jax
import jax.numpy as jnp
from jax import lax

D = 1024
HEADS = 8
HEAD = 128
NODE_DEV = 128
TILE = 128
DEGREE = 4
VIRTUAL = 4
SHARDS = 128
NODES = 16384
GROUP = 1
BLOCKS = 1
TMAX = 3
N_MP = 4


def draw_qkv_weight(key, part):
    key = jax.random.fold_in(key, 41)
    key_base, key_scale = jax.random.split(key, 2)
    column_scale = jnp.exp(jax.random.uniform(key_scale, (1, 3, D), jnp.float32, math.log(0.3), math.log(3.0)))
    base = jax.random.normal(key_base, (D, 3, D), jnp.float32)
    values = base * column_scale / math.sqrt(D)
    return jnp.clip(values, -0.5, 0.5).astype(jnp.bfloat16)


def draw_neighbours(key, part):
    key = jax.random.fold_in(key, 11)
    row_ids = jnp.arange(NODE_DEV, dtype=jnp.int32)
    group_of = row_ids // GROUP
    shard_ids = jnp.arange(SHARDS, dtype=jnp.int32)[:, None]
    results = []
    for perm_index in range(DEGREE):
        perm_key = jax.random.fold_in(key, perm_index)
        key_shift, key_send, key_recv = jax.random.split(perm_key, 3)
        shifts = jax.random.permutation(key_shift, SHARDS).astype(jnp.int32)
        send_perm = jax.vmap(lambda single: jax.random.permutation(single, NODE_DEV))(jax.random.split(key_send, SHARDS)).astype(jnp.int32)
        recv_perm = jax.vmap(lambda single: jax.random.permutation(single, NODE_DEV))(jax.random.split(key_recv, SHARDS)).astype(jnp.int32)
        target_shard = (shard_ids + shifts[group_of][None, :]) % SHARDS
        target = target_shard * NODE_DEV + recv_perm[target_shard, row_ids[None, :]]
        undo_send = jnp.argsort(send_perm, axis=1).astype(jnp.int32)
        placed = jnp.take_along_axis(target, undo_send, axis=1)
        results.append(placed.reshape(-1))
    return jnp.stack(results).astype(jnp.int32)


def draw_tile_list(key, part):
    key = jax.random.fold_in(key, 23)
    span_size = BLOCKS + 2
    pair_ids = jnp.arange(TMAX, dtype=jnp.int32)
    query_block = pair_ids // span_size
    key_block = pair_ids % span_size
    diagonal = key_block == query_block + 1
    lower_rim = (query_block == 0) & (key_block == 0)
    upper_rim = (query_block == BLOCKS - 1) & (key_block == BLOCKS + 1)
    rank_class = jnp.where(diagonal, 0, jnp.where(lower_rim | upper_rim, 1 << 25, 1 << 26))
    noise = jax.random.randint(key, (SHARDS, TMAX), 0, 16384, dtype=jnp.int32)
    ranking = rank_class[None, :] + noise * 256 + pair_ids[None, :]
    picked = jnp.argsort(ranking, axis=1).astype(jnp.int32)
    return jnp.stack([query_block[picked], key_block[picked]], axis=-1).astype(jnp.int32)


def draw_tile_count(key, part):
    key = jax.random.fold_in(key, 37)
    key_spread, key_busy = jax.random.split(key)
    spread = TMAX - BLOCKS - 2
    random_level = jax.random.randint(key_spread, (SHARDS,), 0, spread + 1, dtype=jnp.int32)
    counts = BLOCKS + 2 + random_level * random_level // max(spread, 1)
    busiest = jax.random.randint(key_busy, (), 0, SHARDS, dtype=jnp.int32)
    counts = jnp.where(jnp.arange(SHARDS, dtype=jnp.int32) == busiest, TMAX, counts)
    return counts.astype(jnp.int32)


def touch_ends(entries, own_key, smallest, top_value):
    dims = entries.shape
    index_at = [jax.random.randint(jax.random.fold_in(own_key, axis), (), 0, dims[axis]) for axis in range(len(dims))]
    entries = entries.at[tuple(index_at)].set(smallest)
    longest = dims.index(max(dims))
    index_at[longest] = (index_at[longest] + 1) % dims[longest]
    return entries.at[tuple(index_at)].set(top_value)


def spiked(values, stream_key, source, target, parts, factor):
    owner, partner = [(jnp.arange(values.shape[axis_at]) // (values.shape[axis_at] // parts)).reshape([-1 if axis == axis_at else 1 for axis in range(values.ndim)]) for axis_at in (source, target)]
    chosen = jax.random.permutation(stream_key, parts)[partner]
    strong = (owner == chosen) | (owner == (partner + parts // 2) % parts)
    return jnp.where(strong, factor * values, values)


def shard_levels(stream_key, shape, shards, least, high):
    gain = 1.0
    for position, blocks in shards:
        draws = jax.random.uniform(jax.random.fold_in(jax.random.fold_in(stream_key, 6), position), (blocks,), jnp.float32, least / len(shards), high / len(shards))
        gain = gain * jnp.repeat(jnp.exp(draws), shape[position] // blocks).reshape((-1,) + (1,) * (len(shape) - 1 - position))
    return gain


def gaussian(own_key, shape, deviation, reach, shards=(), kind=jnp.bfloat16):
    drawn = jax.random.normal(own_key, shape, jnp.float32) * deviation
    if len(shards) > 0:
        drawn = shard_levels(own_key, shape, shards, -0.22, 0.18) * drawn
    return jnp.clip(drawn, min=-reach, max=reach).astype(kind)


def noise_with(key, shape, scale, reach, cuts, heavy, kind=jnp.bfloat16):
    drawn = scale * jax.random.normal(key, shape, jnp.float32)
    if cuts:
        drawn = drawn * shard_levels(key, shape, cuts, -0.22, 0.18)
    return jnp.clip(spiked(drawn, jax.random.fold_in(key, 3), *heavy), -reach, reach).astype(kind)


def setup_inputs(seed: int = 0) -> dict:
    streams_of = jax.random.split(jax.random.key(seed), 10)
    return {
        "features": noise_with(streams_of[0], (NODES, D), 1.0, 24.0, ((0, 128),), (0, 1, 128, 5.5)),
        "qkv_weight": draw_qkv_weight(jax.random.fold_in(streams_of[9], 71), 0),
        "vnode_emb": gaussian(streams_of[2], (VIRTUAL, D), 1.0, 6.0),
        "edge_bias": jnp.clip(jax.random.uniform(streams_of[3], (3, HEADS), jnp.float32, -1.0, 1.0) * shard_levels(streams_of[3], (3, HEADS), ((1, 4),), -0.4, 0.0), -1.0, 1.0),
        "out_grad": gaussian(streams_of[4], (NODES, D), 1.0, 6.0, ((0, 128), (1, 4))),
        "neighbours": draw_neighbours(jax.random.fold_in(streams_of[9], 71), 0),
        "member": touch_ends((jax.random.randint(streams_of[6], (NODES, VIRTUAL), 0, 2) < 1).astype(jnp.int32), jax.random.fold_in(streams_of[6], 1), 0, 1),
        "tile_list": draw_tile_list(jax.random.fold_in(streams_of[9], 71), 0),
        "tile_count": draw_tile_count(jax.random.fold_in(streams_of[9], 71), 0),
    }


SHARPNESS = 8.0
EPSILON = 1e-06
PRECISE = lax.Precision.HIGHEST

def unit_rows(values):
    return values * lax.rsqrt(lax.optimization_barrier(jnp.mean(values * values, axis=-1, keepdims=True)) + EPSILON)

def split_heads(values):
    return values.reshape(values.shape[:-1] + (values.shape[-1] // HEAD, HEAD))

def tile_mask(listing, how_many):
    span_size = BLOCKS + 2
    listed = jnp.arange(listing.shape[0]) < how_many
    codes = listing[:, 0] * span_size + listing[:, 1]
    places = jnp.arange(BLOCKS * span_size)
    allowed = jnp.any((codes[None, :] == places[:, None]) & listed[None, :], axis=1)
    allowed = allowed.reshape(BLOCKS, span_size)
    return jnp.repeat(jnp.repeat(allowed, TILE, axis=0), TILE, axis=1).astype(jnp.float32)

def attend(query_rows, extended, nearby, virtual_rows, mask, members, edge_bias):
    score_scale = SHARPNESS / HEAD
    log_boost = math.log(TILE)
    unit_q = unit_rows(split_heads(query_rows))
    unit_k = unit_rows(split_heads(extended[:, 0]))
    values_ext = split_heads(extended[:, 1])
    weights = jnp.exp(score_scale * jnp.einsum('qhd,khd->hqk', unit_q, unit_k, precision=PRECISE) + edge_bias[0][:, None, None]) * mask[None]
    totals = lax.optimization_barrier(jnp.sum(weights, axis=2)).T
    mixture = jnp.einsum('hqk,khd->qhd', weights, values_ext, precision=PRECISE)
    unit_near = unit_rows(split_heads(nearby[:, :, 0]))
    values_near = split_heads(nearby[:, :, 1])
    near_weights = jnp.exp(score_scale * lax.optimization_barrier(jnp.sum(unit_q[None] * unit_near, axis=-1)) + edge_bias[1] + log_boost)
    totals = totals + lax.optimization_barrier(jnp.sum(near_weights, axis=0))
    mixture = mixture + lax.optimization_barrier(jnp.sum(near_weights[..., None] * values_near, axis=0))
    unit_virtual = unit_rows(split_heads(virtual_rows[:, 0]))
    values_virtual = split_heads(virtual_rows[:, 1])
    virtual_weights = jnp.exp(score_scale * jnp.einsum('rhd,vhd->rhv', unit_q, unit_virtual, precision=PRECISE) + edge_bias[2][None, :, None] + log_boost) * members[:, None, :]
    totals = totals + lax.optimization_barrier(jnp.sum(virtual_weights, axis=2))
    mixture = mixture + jnp.einsum('rhv,vhd->rhd', virtual_weights, values_virtual, precision=PRECISE)
    result = mixture / totals[..., None]
    return result.reshape(result.shape[0], -1)

def reference(features, qkv_weight, vnode_emb, edge_bias, out_grad, neighbours, member, tile_list, tile_count):
    flat_weight = qkv_weight.reshape(D, 3 * D)
    projected = jnp.dot(features, flat_weight, preferred_element_type=jnp.float32).reshape(NODES, 3, D)
    query = projected[:, 0]
    rounded = lax.optimization_barrier(projected[:, 1:].astype(jnp.bfloat16)).astype(jnp.float32)
    kv_weight = qkv_weight[:, 1:].reshape(D, 2 * D)
    virtual_kv = jnp.dot(vnode_emb, kv_weight, preferred_element_type=jnp.float32).reshape(VIRTUAL, 2, D)
    members = member.astype(jnp.float32)
    offsets = jnp.arange(NODE_DEV + 2 * TILE, dtype=jnp.int32) - TILE

    def shard_step(carried, shard_index):
        near_total, virtual_total = carried
        first_row = (shard_index * NODE_DEV).astype(jnp.int32)
        query_rows = lax.dynamic_slice_in_dim(query, first_row, NODE_DEV, 0)
        ext_index = ((first_row + offsets) % NODES).astype(jnp.int32)
        extended = rounded[ext_index]
        near_index = lax.dynamic_slice_in_dim(neighbours, first_row, NODE_DEV, 1)
        nearby = rounded[near_index]
        grad_rows = lax.dynamic_slice_in_dim(out_grad, first_row, NODE_DEV, 0).astype(jnp.float32)
        member_rows = lax.dynamic_slice_in_dim(members, first_row, NODE_DEV, 0)
        mask = tile_mask(tile_list[shard_index], tile_count[shard_index])

        def local_attend(q_part, e_part, n_part, v_part):
            return attend(q_part, e_part, n_part, v_part, mask, member_rows, edge_bias)
        output_rows, pull_back = jax.vjp(local_attend, query_rows, extended, nearby, virtual_kv)
        d_query, d_extended, d_nearby, d_virtual = pull_back(grad_rows)
        near_round = lax.optimization_barrier(d_nearby.astype(jnp.bfloat16)).astype(jnp.float32)
        near_total = near_total.at[near_index.reshape(-1)].add(near_round.reshape(-1, 2, D))
        core_part = d_extended[TILE:TILE + NODE_DEV]
        left_rim = d_extended[:TILE]
        right_rim = d_extended[TILE + NODE_DEV:]
        return ((near_total, virtual_total + d_virtual), (d_query, core_part, left_rim, right_rim))
    start_state = (jnp.zeros((NODES, 2, D), jnp.float32), jnp.zeros((VIRTUAL, 2, D), jnp.float32))
    final_state, outputs = lax.scan(shard_step, start_state, jnp.arange(SHARDS, dtype=jnp.int32))
    near_total, virtual_total = final_state
    d_queries, cores, lefts, rights = outputs
    cores = cores.at[:, NODE_DEV - TILE:].add(jnp.roll(lefts, -1, axis=0))
    cores = cores.at[:, :TILE].add(jnp.roll(rights, 1, axis=0))
    kv_total = cores.reshape(NODES, 2, D) + near_total
    d_queries = d_queries.reshape(NODES, D)
    gradient_qkv = jnp.concatenate([d_queries[:, None], kv_total], axis=1).astype(jnp.bfloat16)
    width_part = D // N_MP
    summed = jnp.zeros((NODES, D), jnp.float32)
    for group_index in range(N_MP):
        low_column = group_index * width_part
        grad_part = gradient_qkv[:, :, low_column:low_column + width_part].reshape(NODES, 3 * width_part)
        weight_part = qkv_weight[:, :, low_column:low_column + width_part].reshape(D, 3 * width_part)
        partial_sum = jnp.dot(grad_part, weight_part.T, preferred_element_type=jnp.float32)
        summed = summed + lax.optimization_barrier(partial_sum.astype(jnp.bfloat16)).astype(jnp.float32)
    feature_grad = summed.astype(jnp.bfloat16)
    out_scale = 1.0 / math.sqrt(NODES)
    weight_main = jnp.dot(features.T, gradient_qkv.reshape(NODES, 3 * D), preferred_element_type=jnp.float32).reshape(D, 3, D)
    weight_extra = jnp.einsum('vd,vtc->dtc', vnode_emb.astype(jnp.float32), virtual_total, precision=PRECISE)
    weight_grad = (weight_main + jnp.concatenate([jnp.zeros_like(weight_extra[:, :1]), weight_extra], axis=1)) * out_scale
    vnode_grad = jnp.einsum('vtc,dtc->vd', virtual_total, qkv_weight[:, 1:].astype(jnp.float32), precision=PRECISE) * out_scale
    return (feature_grad, weight_grad, vnode_grad)
```

```python
import math

import jax
import jax.numpy as jnp
from jax import lax
from jax.experimental import pallas as pl
from jax.experimental.pallas import tpu as pltpu
from jax.sharding import Mesh
from jax.sharding import PartitionSpec as P

HEAD = 128
TILE = 128
DEGREE = 4
VIRTUAL = 4
ROWS = 128
SHARDS = 128
COLS = 256
HEADS_DEV = 2
SIZES = {"z": 16, "x": 4, "c": 2, "mp": 4}
NODES = ("z", "x", "c")

SHARPNESS = 8.0
EPSILON = 1e-06
SCALE = SHARPNESS / HEAD
BOOST = math.log(TILE)
PRECISE = lax.Precision.HIGHEST
F32 = jnp.float32
BF16 = jnp.bfloat16

NN = (((1,), (0,)), ((), ()))
NT = (((1,), (1,)), ((), ()))
TN = (((0,), (0,)), ((), ()))


def mul(left, right, dims, precision=None):
    return lax.dot_general(left, right, dims, precision=precision, preferred_element_type=F32)


def unit(values):
    inv = lax.rsqrt(jnp.mean(values * values, axis=-1, keepdims=True) + EPSILON)
    return values * inv, inv


def unit_back(rows, inv, cotangent):
    return inv * (cotangent - rows * jnp.mean(rows * cotangent, axis=-1, keepdims=True))


def head_of(ref, head, part=0):
    start = part * COLS + head * HEAD
    return ref[:, start : start + HEAD]


def owner_hits(owners_ref, perm):
    shard = lax.broadcasted_iota(jnp.int32, (SHARDS, ROWS), 0)
    return jnp.where(shard == owners_ref[perm : perm + 1, :], 1.0, 0.0).astype(BF16)


def asked_hits(asked_ref, perm):
    row = lax.broadcasted_iota(jnp.int32, (SHARDS, ROWS), 1)
    return jnp.where(row == asked_ref[:, perm : perm + 1], 1.0, 0.0).astype(BF16)


def serve_kernel(asked_ref, kv_ref, out_ref):
    kv = kv_ref[...]
    for perm in range(DEGREE):
        picked = mul(asked_hits(asked_ref, perm), kv, NN)
        out_ref[:, perm * 2 * COLS : (perm + 1) * 2 * COLS] = picked.astype(BF16)


def virtual_weights(bias_ref, head, unit_q, virtual_ref, member_ref):
    unit_v, inv_v = unit(head_of(virtual_ref, head))
    scores = SCALE * mul(unit_q, unit_v, NT, PRECISE) + bias_ref[2, head] + BOOST
    return jnp.exp(scores) * member_ref[...].astype(F32), unit_v, inv_v


def local_kernel(bias_ref, query_ref, left_ref, own_ref, right_ref, grad_ref, virtual_ref, member_ref, out_ref):
    columns = []
    for head in range(HEADS_DEV):
        unit_q, _ = unit(head_of(query_ref, head))
        query = unit_q.astype(BF16)
        grad = head_of(grad_ref, head)
        total = jnp.zeros((ROWS, 1), F32)
        mixed = jnp.zeros((ROWS, 1), F32)
        for block in (left_ref, own_ref, right_ref):
            unit_k, _ = unit(head_of(block, head).astype(F32))
            weights = jnp.exp(SCALE * mul(query, unit_k.astype(BF16), NT) + bias_ref[0, head])
            grads = mul(grad, head_of(block, head, 1), NT)
            total += jnp.sum(weights, axis=1, keepdims=True)
            mixed += jnp.sum(weights * grads, axis=1, keepdims=True)
        weights, _, _ = virtual_weights(bias_ref, head, unit_q, virtual_ref, member_ref)
        grads = mul(grad.astype(F32), head_of(virtual_ref, head, 1), NT, PRECISE)
        total += jnp.sum(weights, axis=1, keepdims=True)
        mixed += jnp.sum(weights * grads, axis=1, keepdims=True)
        columns += [total, mixed]
    out_ref[...] = jnp.concatenate(columns, axis=1)


def near_kernel(bias_ref, owners_ref, query_ref, near_ref, grad_ref, sums_ref, send_ref, stats_ref, dquery_ref):
    totals = [sums_ref[:, 2 * head : 2 * head + 1] for head in range(HEADS_DEV)]
    mixed = [sums_ref[:, 2 * head + 1 : 2 * head + 2] for head in range(HEADS_DEV)]
    unit_q = [unit(head_of(query_ref, head))[0] for head in range(HEADS_DEV)]
    grad = [head_of(grad_ref, head).astype(F32) for head in range(HEADS_DEV)]
    saved = {}
    for perm in range(DEGREE):
        hits = owner_hits(owners_ref, perm)
        rows = mul(hits, near_ref[:, perm * 2 * COLS : (perm + 1) * 2 * COLS], TN)
        for head in range(HEADS_DEV):
            unit_k, inv_k = unit(rows[:, head * HEAD : (head + 1) * HEAD])
            values = rows[:, COLS + head * HEAD : COLS + (head + 1) * HEAD]
            scores = SCALE * jnp.sum(unit_q[head] * unit_k, axis=1, keepdims=True)
            weights = jnp.exp(scores + bias_ref[1, head] + BOOST)
            grads = jnp.sum(grad[head] * values, axis=1, keepdims=True)
            totals[head] = totals[head] + weights
            mixed[head] = mixed[head] + weights * grads
            saved[perm, head] = (unit_k, inv_k, weights, grads)
    inverse = [1.0 / total for total in totals]
    delta = [mixed[head] * inverse[head] for head in range(HEADS_DEV)]
    dquery = [jnp.zeros((ROWS, HEAD), F32) for _ in range(HEADS_DEV)]
    for perm in range(DEGREE):
        dkeys, dvalues = [], []
        for head in range(HEADS_DEV):
            unit_k, inv_k, weights, grads = saved[perm, head]
            probs = weights * inverse[head]
            dscores = probs * (grads - delta[head]) * SCALE
            dquery[head] = dquery[head] + dscores * unit_k
            dkeys.append(unit_back(unit_k, inv_k, dscores * unit_q[head]).astype(BF16))
            dvalues.append((probs * grad[head]).astype(BF16))
        picked = mul(owner_hits(owners_ref, perm), jnp.concatenate(dkeys + dvalues, axis=1), NN)
        send_ref[:, perm * 2 * COLS : (perm + 1) * 2 * COLS] = picked.astype(BF16)
    stats_ref[...] = jnp.concatenate([inverse[0], delta[0], inverse[1], delta[1]], axis=1)
    dquery_ref[...] = jnp.concatenate(dquery, axis=1)


def back_kernel(
    bias_ref, query_ref, left_ref, own_ref, right_ref, grad_ref, virtual_ref, member_ref, stats_ref, dnear_ref,
    dquery_ref, dleft_ref, down_ref, dright_ref, dvirtual_ref,
):
    for head in range(HEADS_DEV):
        unit_q, inv_q = unit(head_of(query_ref, head))
        query = unit_q.astype(BF16)
        grad = head_of(grad_ref, head)
        inverse = stats_ref[:, 2 * head : 2 * head + 1]
        delta = stats_ref[:, 2 * head + 1 : 2 * head + 2]
        dquery = head_of(dnear_ref, head)
        keys_at = slice(head * HEAD, (head + 1) * HEAD)
        values_at = slice(COLS + head * HEAD, COLS + (head + 1) * HEAD)
        for block, out in ((left_ref, dleft_ref), (own_ref, down_ref), (right_ref, dright_ref)):
            unit_k, inv_k = unit(head_of(block, head).astype(F32))
            keys = unit_k.astype(BF16)
            probs = jnp.exp(SCALE * mul(query, keys, NT) + bias_ref[0, head]) * inverse
            grads = mul(grad, head_of(block, head, 1), NT)
            dscores = (probs * (grads - delta) * SCALE).astype(BF16)
            dquery += mul(dscores, keys, NN)
            out[:, keys_at] = unit_back(unit_k, inv_k, mul(dscores, query, TN)).astype(out.dtype)
            out[:, values_at] = mul(probs.astype(BF16), grad, TN).astype(out.dtype)
        weights, unit_v, inv_v = virtual_weights(bias_ref, head, unit_q, virtual_ref, member_ref)
        probs = weights * inverse
        wide = grad.astype(F32)
        grads = mul(wide, head_of(virtual_ref, head, 1), NT, PRECISE)
        dscores = probs * (grads - delta) * SCALE
        dquery += mul(dscores, unit_v, NN, PRECISE)
        dvirtual_ref[:, keys_at] = unit_back(unit_v, inv_v, mul(dscores, unit_q, TN, PRECISE))
        dvirtual_ref[:, values_at] = mul(probs, wide, TN, PRECISE)
        dquery_ref[:, keys_at] = unit_back(unit_q, inv_q, dquery).astype(BF16)


def total_kernel(asked_ref, back_ref, dquery_ref, down_ref, from_left_ref, from_right_ref, out_ref):
    total = down_ref[...] + from_left_ref[...].astype(F32) + from_right_ref[...].astype(F32)
    for perm in range(DEGREE):
        total += mul(asked_hits(asked_ref, perm), back_ref[:, perm * 2 * COLS : (perm + 1) * 2 * COLS], TN)
    out_ref[:, :COLS] = dquery_ref[...]
    out_ref[:, COLS:] = total.astype(BF16)


VMEM = pl.BlockSpec(memory_space=pltpu.VMEM)
SMEM = pl.BlockSpec(memory_space=pltpu.SMEM)


def call(kernel, outs, *args, scalars=0, flops=10**8):
    shapes = [jax.ShapeDtypeStruct(shape, kind) for shape, kind in outs]
    moved = sum(math.prod(a.shape) * a.dtype.itemsize for a in [*args, *shapes])
    return pl.pallas_call(
        kernel,
        out_shape=shapes,
        in_specs=[SMEM] * scalars + [VMEM] * (len(args) - scalars),
        out_specs=[VMEM] * len(shapes),
        compiler_params=pltpu.CompilerParams(vmem_limit_bytes=32 * 2**20),
        cost_estimate=pl.CostEstimate(flops=flops, bytes_accessed=moved, transcendentals=0),
    )(*args)


def exchange(values, axis):
    return lax.all_to_all(values, axis, split_axis=0, concat_axis=0, tiled=True)


def shift(values, axis, step):
    count = math.prod(SIZES[name] for name in axis) if isinstance(axis, tuple) else SIZES[axis]
    return lax.ppermute(values, axis, [(i, (i + step) % count) for i in range(count)])


def swap(values, axis, bit):
    return lax.ppermute(values, axis, [(i, i ^ bit) for i in range(SIZES[axis])])


def two_terms(values):
    high = values.astype(BF16)
    return high, (values - high.astype(F32)).astype(BF16)


def body(features, qkv_weight, vnode_emb, edge_bias, out_grad, neighbours, member, tile_list, tile_count):
    width_in = qkv_weight.shape[0]
    with jax.named_scope("ask"):
        owners = neighbours // ROWS
        hit = owners[:, None, :] == jnp.arange(SHARDS, dtype=jnp.int32)[None, :, None]
        wanted = jnp.sum(jnp.where(hit, (neighbours % ROWS)[:, None, :], 0), axis=2)
        asked = exchange(wanted.T, NODES)
    with jax.named_scope("project"):
        flat_weight = qkv_weight.reshape(width_in, 3 * COLS)
        projected = jnp.dot(features, flat_weight, preferred_element_type=F32)
        query = projected[:, :COLS]
        kv = projected[:, COLS:].astype(BF16)
        virtual_kv = jnp.dot(vnode_emb, flat_weight[:, COLS:], preferred_element_type=F32)
        from_left = shift(kv, NODES, 1)
        from_right = shift(kv, NODES, -1)
    with jax.named_scope("select"):
        core = lax.axis_index("c")
        place = jnp.arange(width_in, dtype=jnp.int32)
        half, rest = place // 512, place % 512
        source = (rest // 8 % 16) * 64 + (rest // 128) * 16 + (half ^ core) * 8 + rest % 8
        chosen = (jnp.arange(width_in, dtype=jnp.int32)[:, None] == source[None, :]).astype(BF16)
        sorted_in = jnp.dot(jnp.concatenate([features, vnode_emb], axis=0), chosen, preferred_element_type=F32)
        sorted_in = sorted_in.astype(BF16)
        other_in = swap(sorted_in[:ROWS, 512:], "c", 1)
        wide_in = jnp.concatenate([sorted_in[:ROWS, :512], other_in, sorted_in[ROWS:, :512], sorted_in[ROWS:, :512]], axis=0)
    with jax.named_scope("serve"):
        served, = call(serve_kernel, [((SHARDS, DEGREE * 2 * COLS), BF16)], asked, kv)
        near = exchange(served, NODES)
    with jax.named_scope("local"):
        sums, = call(
            local_kernel, [((ROWS, 4), F32)],
            edge_bias, query, from_left, kv, from_right, out_grad, virtual_kv, member, scalars=1,
        )
    with jax.named_scope("near"):
        send, stats, dnear = call(
            near_kernel, [((SHARDS, DEGREE * 2 * COLS), BF16), ((ROWS, 4), F32), ((ROWS, COLS), F32)],
            edge_bias, owners, query, near, out_grad, sums, scalars=1,
        )
        back = exchange(send, NODES)
    with jax.named_scope("back"):
        dquery, dleft, down, dright, dvirtual = call(
            back_kernel,
            [((ROWS, COLS), BF16), ((ROWS, 2 * COLS), BF16), ((ROWS, 2 * COLS), F32), ((ROWS, 2 * COLS), BF16), ((VIRTUAL, 2 * COLS), F32)],
            edge_bias, query, from_left, kv, from_right, out_grad, virtual_kv, member, stats, dnear, scalars=1,
        )
        back_left = shift(dright, NODES, 1)
        back_right = shift(dleft, NODES, -1)
    with jax.named_scope("virtual"):
        high, low = two_terms(dvirtual)
        kv_weight = flat_weight[:, COLS:]
        vnode = mul(jnp.concatenate([high, low], axis=0), kv_weight, NT)
        vnode = vnode[:VIRTUAL] + vnode[VIRTUAL:]
        for axis, bit in (("mp", 1), ("mp", 2), ("c", 1), ("x", 1), ("x", 2)):
            vnode = vnode + swap(vnode, axis, bit)
        dvirtual = dvirtual + swap(dvirtual, "c", 1)
        high, low = two_terms(dvirtual)
        extra = jnp.concatenate([high, low], axis=0)
        extra = jnp.concatenate([jnp.zeros((2 * VIRTUAL, COLS), BF16), extra], axis=1)
    with jax.named_scope("total"):
        dqkv, = call(
            total_kernel, [((ROWS, 3 * COLS), BF16)],
            asked, back, dquery, down, back_left, back_right,
        )
        other = swap(dqkv, "c", 1)
    with jax.named_scope("feature"):
        partial = mul(dqkv, flat_weight, NT).astype(BF16)
        me = lax.axis_index("mp")
        summed = lax.dynamic_slice_in_dim(partial, me * COLS, COLS, 1).astype(F32)
        for step in range(1, 4):
            piece = lax.dynamic_slice_in_dim(partial, ((me + step) % 4) * COLS, COLS, 1)
            summed = summed + shift(piece, "mp", step).astype(F32)
        feature_grad = summed.astype(BF16)
    with jax.named_scope("weight"):
        wide_out = jnp.concatenate([dqkv, other, extra], axis=0)
        term = mul(wide_in, wide_out, TN).astype(BF16)
        term = exchange(term.reshape(4, 128, 3 * COLS), "x")
        term = jnp.sum(term.astype(F32), axis=0).reshape(16, 8, 3 * COLS)
        tail = jnp.broadcast_to(vnode.reshape(1, 8, 512), (16, 8, 512))
        term = jnp.concatenate([term, tail], axis=2).astype(BF16)
        term = jnp.sum(exchange(term, "z").astype(F32), axis=0)
        out_scale = 1.0 / math.sqrt(ROWS * SHARDS)
        weight_grad = (term[:, : 3 * COLS] * out_scale).reshape(8, 3, COLS)
        vnode_grad = (term[:, 3 * COLS :] * out_scale).reshape(VIRTUAL, width_in)
    return feature_grad, weight_grad, vnode_grad


def solution(mesh):
    fine = Mesh(mesh.devices.reshape(tuple(SIZES.values())), tuple(SIZES))
    return jax.shard_map(
        body,
        mesh=fine,
        in_specs=(
            P(NODES, None),
            P(None, None, "mp"),
            P(),
            P(None, "mp"),
            P(NODES, "mp"),
            P(None, NODES),
            P(NODES, None),
            P(NODES, None, None),
            P(NODES),
        ),
        out_specs=(P(NODES, "mp"), P(NODES, None, "mp"), P()),
        check_vma=False,
    )
```

```python
import math

import jax
import jax.numpy as jnp
from jax import lax
from jax.experimental import pallas as pl
from jax.experimental.pallas import tpu as pltpu
from jax.sharding import Mesh
from jax.sharding import PartitionSpec as P

HEAD = 128
TILE = 128
DEGREE = 4
VIRTUAL = 4
ROWS = 128
SHARDS = 128
COLS = 256
HEADS_DEV = 2
SLOTS = 2 * DEGREE
SIZES = {"z": 16, "x": 4, "c": 2, "mp": 4}
NODES = ("z", "x", "c")

SHARPNESS = 8.0
EPSILON = 1e-06
SCALE = SHARPNESS / HEAD
BOOST = math.log(TILE)
PRECISE = lax.Precision.HIGHEST
F32 = jnp.float32
BF16 = jnp.bfloat16

NN = (((1,), (0,)), ((), ()))
NT = (((1,), (1,)), ((), ()))
TN = (((0,), (0,)), ((), ()))


def mul(left, right, dims, precision=None):
    return lax.dot_general(left, right, dims, precision=precision, preferred_element_type=F32)


def unit(values):
    inv = lax.rsqrt(jnp.mean(values * values, axis=-1, keepdims=True) + EPSILON)
    return values * inv, inv


def unit_back(rows, inv, cotangent):
    return inv * (cotangent - rows * jnp.mean(rows * cotangent, axis=-1, keepdims=True))


def head_of(ref, head, part=0):
    start = part * COLS + head * HEAD
    return ref[:, start : start + HEAD]


def ones_where(condition):
    return jnp.where(condition, 1.0, 0.0).astype(BF16)


def serve_kernel(asked_ref, kv_ref, out_ref):
    asked = asked_ref[:, 0, :].astype(F32).astype(BF16)
    place = lax.broadcasted_iota(jnp.int32, (SHARDS * SLOTS, SHARDS), 0)
    shard = lax.broadcasted_iota(jnp.int32, (SHARDS * SLOTS, SHARDS), 1)
    spread = mul(ones_where(place // SLOTS == shard), asked, NN)
    own_slot = lax.broadcasted_iota(jnp.int32, spread.shape, 0) % SLOTS
    slot = lax.broadcasted_iota(jnp.int32, spread.shape, 1)
    row = jnp.sum(jnp.where(slot == own_slot, spread, 0.0), axis=1, keepdims=True).astype(jnp.int32)
    hits = ones_where(lax.broadcasted_iota(jnp.int32, (SHARDS * SLOTS, 2 * ROWS), 1) == row)
    rows = jnp.concatenate([kv_ref[:, :COLS], kv_ref[:, COLS:]], axis=0)
    out_ref[...] = mul(hits, rows, NN).astype(BF16)


def virtual_weights(bias_ref, head, unit_q, virtual_ref, member_ref):
    unit_v, inv_v = unit(head_of(virtual_ref, head))
    scores = SCALE * mul(unit_q, unit_v, NT, PRECISE) + bias_ref[2, head] + BOOST
    return jnp.exp(scores) * member_ref[...].astype(F32), unit_v, inv_v


def local_kernel(bias_ref, query_ref, left_ref, own_ref, right_ref, grad_ref, virtual_ref, member_ref, out_ref):
    columns = []
    for head in range(HEADS_DEV):
        unit_q, _ = unit(head_of(query_ref, head))
        query = unit_q.astype(BF16)
        grad = head_of(grad_ref, head)
        total = jnp.zeros((ROWS, 1), F32)
        mixed = jnp.zeros((ROWS, 1), F32)
        for block in (left_ref, own_ref, right_ref):
            unit_k, _ = unit(head_of(block, head).astype(F32))
            weights = jnp.exp(SCALE * mul(query, unit_k.astype(BF16), NT) + bias_ref[0, head])
            grads = mul(grad, head_of(block, head, 1), NT)
            total += jnp.sum(weights, axis=1, keepdims=True)
            mixed += jnp.sum(weights * grads, axis=1, keepdims=True)
        weights, _, _ = virtual_weights(bias_ref, head, unit_q, virtual_ref, member_ref)
        grads = mul(grad.astype(F32), head_of(virtual_ref, head, 1), NT, PRECISE)
        total += jnp.sum(weights, axis=1, keepdims=True)
        mixed += jnp.sum(weights * grads, axis=1, keepdims=True)
        columns += [total, mixed]
    out_ref[...] = jnp.concatenate(columns, axis=1)


def near_kernel(bias_ref, columns_ref, codes_ref, query_ref, near_ref, grad_ref, sums_ref, send_ref, stats_ref, dquery_ref, pieces):
    totals = [sums_ref[:, 2 * head : 2 * head + 1] for head in range(HEADS_DEV)]
    mixed = [sums_ref[:, 2 * head + 1 : 2 * head + 2] for head in range(HEADS_DEV)]
    place = lax.broadcasted_iota(jnp.int32, (ROWS, SHARDS * SLOTS), 1)
    received = near_ref[...]
    unit_q = [unit(head_of(query_ref, head))[0] for head in range(HEADS_DEV)]
    grad = [head_of(grad_ref, head).astype(F32) for head in range(HEADS_DEV)]
    saved = {}
    for perm in range(DEGREE):
        key_rows = mul(ones_where(place == columns_ref[:, 2 * perm : 2 * perm + 1]), received, NN)
        value_rows = mul(ones_where(place == columns_ref[:, 2 * perm + 1 : 2 * perm + 2]), received, NN)
        for head in range(HEADS_DEV):
            unit_k, inv_k = unit(key_rows[:, head * HEAD : (head + 1) * HEAD])
            values = value_rows[:, head * HEAD : (head + 1) * HEAD]
            scores = SCALE * jnp.sum(unit_q[head] * unit_k, axis=1, keepdims=True)
            weights = jnp.exp(scores + bias_ref[1, head] + BOOST)
            grads = jnp.sum(grad[head] * values, axis=1, keepdims=True)
            totals[head] = totals[head] + weights
            mixed[head] = mixed[head] + weights * grads
            saved[perm, head] = (unit_k, inv_k, weights, grads)
    inverse = [1.0 / total for total in totals]
    delta = [mixed[head] * inverse[head] for head in range(HEADS_DEV)]
    dquery = [jnp.zeros((ROWS, HEAD), F32) for _ in range(HEADS_DEV)]
    for perm in range(DEGREE):
        for head in range(HEADS_DEV):
            unit_k, inv_k, weights, grads = saved[perm, head]
            probs = weights * inverse[head]
            dscores = probs * (grads - delta[head]) * SCALE
            dquery[head] = dquery[head] + dscores * unit_k
            at = slice(head * HEAD, (head + 1) * HEAD)
            keys_at = slice(2 * perm * ROWS, (2 * perm + 1) * ROWS)
            values_at = slice((2 * perm + 1) * ROWS, (2 * perm + 2) * ROWS)
            pieces[keys_at, at] = unit_back(unit_k, inv_k, dscores * unit_q[head]).astype(BF16)
            pieces[values_at, at] = (probs * grad[head]).astype(BF16)
    returned = pieces[...]
    for block in range(SLOTS):
        place = lax.broadcasted_iota(jnp.int32, (ROWS, SLOTS * ROWS), 0) + block * ROWS
        send_ref[block * ROWS : (block + 1) * ROWS, :] = mul(ones_where(place == codes_ref[...]), returned, NN).astype(BF16)
    stats_ref[...] = jnp.concatenate([inverse[0], delta[0], inverse[1], delta[1]], axis=1)
    dquery_ref[...] = jnp.concatenate(dquery, axis=1)


def back_kernel(
    bias_ref, query_ref, left_ref, own_ref, right_ref, grad_ref, virtual_ref, member_ref, stats_ref, dnear_ref,
    dquery_ref, dleft_ref, down_ref, dright_ref, dvirtual_ref,
):
    for head in range(HEADS_DEV):
        unit_q, inv_q = unit(head_of(query_ref, head))
        query = unit_q.astype(BF16)
        grad = head_of(grad_ref, head)
        inverse = stats_ref[:, 2 * head : 2 * head + 1]
        delta = stats_ref[:, 2 * head + 1 : 2 * head + 2]
        dquery = head_of(dnear_ref, head)
        keys_at = slice(head * HEAD, (head + 1) * HEAD)
        values_at = slice(COLS + head * HEAD, COLS + (head + 1) * HEAD)
        for block, out in ((left_ref, dleft_ref), (own_ref, down_ref), (right_ref, dright_ref)):
            unit_k, inv_k = unit(head_of(block, head).astype(F32))
            keys = unit_k.astype(BF16)
            probs = jnp.exp(SCALE * mul(query, keys, NT) + bias_ref[0, head]) * inverse
            grads = mul(grad, head_of(block, head, 1), NT)
            dscores = (probs * (grads - delta) * SCALE).astype(BF16)
            dquery += mul(dscores, keys, NN)
            out[:, keys_at] = unit_back(unit_k, inv_k, mul(dscores, query, TN)).astype(out.dtype)
            out[:, values_at] = mul(probs.astype(BF16), grad, TN).astype(out.dtype)
        weights, unit_v, inv_v = virtual_weights(bias_ref, head, unit_q, virtual_ref, member_ref)
        probs = weights * inverse
        wide = grad.astype(F32)
        grads = mul(wide, head_of(virtual_ref, head, 1), NT, PRECISE)
        dscores = probs * (grads - delta) * SCALE
        dquery += mul(dscores, unit_v, NN, PRECISE)
        dvirtual_ref[:, keys_at] = unit_back(unit_v, inv_v, mul(dscores, unit_q, TN, PRECISE))
        dvirtual_ref[:, values_at] = mul(probs, wide, TN, PRECISE)
        dquery_ref[:, keys_at] = unit_back(unit_q, inv_q, dquery).astype(BF16)


def total_kernel(asked_ref, back_ref, dquery_ref, down_ref, from_left_ref, from_right_ref, tail_ref, out_ref):
    place = lax.broadcasted_iota(jnp.int32, (2 * ROWS, SHARDS * SLOTS), 0)
    near = mul(ones_where(place == asked_ref[...]), back_ref[...], NN)
    rim = from_left_ref[...].astype(F32) + from_right_ref[...].astype(F32)
    total = down_ref[...] + rim
    out_ref[:ROWS, :COLS] = dquery_ref[...]
    out_ref[:ROWS, COLS : 2 * COLS] = (total[:, :COLS] + near[:ROWS]).astype(BF16)
    out_ref[:ROWS, 2 * COLS :] = (total[:, COLS:] + near[ROWS:]).astype(BF16)
    out_ref[ROWS:, :] = tail_ref[...]


def weight_kernel(in_own_ref, in_other_ref, own_ref, other_ref, out_ref):
    own, other = own_ref[...], other_ref[...]
    vnode = own[ROWS + 16 :].astype(F32) + other[ROWS + 16 :].astype(F32)
    high, low = two_terms(vnode[:8] + vnode[8:])
    tail = jnp.concatenate([high.astype(F32), low.astype(F32)], axis=0).astype(BF16)
    for part in range(4):
        at = slice(part * 128, (part + 1) * 128)
        term = mul(in_own_ref[at, :], own, NN) + mul(in_other_ref[at, :], other, NN)
        out_ref[part, :128, :] = term.astype(BF16)
        out_ref[part, 128:, :] = tail


VMEM = pl.BlockSpec(memory_space=pltpu.VMEM)
SMEM = pl.BlockSpec(memory_space=pltpu.SMEM)


def call(kernel, outs, *args, scalars=0, scratch=(), flops=10**8):
    shapes = [jax.ShapeDtypeStruct(shape, kind) for shape, kind in outs]
    moved = sum(math.prod(a.shape) * a.dtype.itemsize for a in [*args, *shapes])
    return pl.pallas_call(
        kernel,
        out_shape=shapes,
        in_specs=[SMEM] * scalars + [VMEM] * (len(args) - scalars),
        out_specs=[VMEM] * len(shapes),
        scratch_shapes=list(scratch),
        compiler_params=pltpu.CompilerParams(vmem_limit_bytes=32 * 2**20),
        cost_estimate=pl.CostEstimate(flops=flops, bytes_accessed=moved, transcendentals=0),
    )(*args)


def exchange(values, axis):
    return lax.all_to_all(values, axis, split_axis=0, concat_axis=0, tiled=True)


def shift(values, axis, step):
    count = math.prod(SIZES[name] for name in axis) if isinstance(axis, tuple) else SIZES[axis]
    return lax.ppermute(values, axis, [(i, (i + step) % count) for i in range(count)])


def swap(values, axis, bit):
    return lax.ppermute(values, axis, [(i, i ^ bit) for i in range(SIZES[axis])])


def two_terms(values):
    high = values.astype(BF16)
    return high, (values - high.astype(F32)).astype(BF16)


def body(features, qkv_weight, vnode_emb, edge_bias, out_grad, neighbours, member, tile_list, tile_count):
    width_in = qkv_weight.shape[0]
    with jax.named_scope("ask"):
        owners = neighbours // ROWS
        hit = owners[:, None, :] == jnp.arange(SHARDS, dtype=jnp.int32)[None, :, None]
        wanted = jnp.sum(jnp.where(hit, (neighbours % ROWS)[:, None, :], 0), axis=2)
        wanted = jnp.stack([wanted, wanted + ROWS], axis=1).reshape(SLOTS, SHARDS)
        asked = exchange(wanted.T.reshape(SHARDS, 1, SLOTS), NODES)
        codes = jnp.repeat(owners, 2, axis=0) * SLOTS + jnp.arange(SLOTS, dtype=jnp.int32)[:, None]
    with jax.named_scope("project"):
        flat_weight = qkv_weight.reshape(width_in, 3 * COLS)
        projected = jnp.dot(features, flat_weight, preferred_element_type=F32)
        query = projected[:, :COLS]
        kv = projected[:, COLS:].astype(BF16)
        virtual_kv = jnp.dot(vnode_emb, flat_weight[:, COLS:], preferred_element_type=F32)
        from_left = shift(kv, NODES, 1)
        from_right = shift(kv, NODES, -1)
    with jax.named_scope("select"):
        core = lax.axis_index("c")
        place = jnp.arange(width_in, dtype=jnp.int32)
        half, rest = place // 512, place % 512
        source = (rest // 8 % 16) * 64 + (rest // 128) * 16 + (half ^ core) * 8 + rest % 8
        chosen = (source[:, None] == jnp.arange(width_in, dtype=jnp.int32)[None, :]).astype(BF16)
        rows_in = jnp.concatenate([features, vnode_emb, vnode_emb, jnp.zeros((24, width_in), BF16)], axis=0)
        sorted_in = mul(chosen, rows_in, NT).astype(BF16)
        in_own = sorted_in[:512]
        in_other = jnp.concatenate([swap(sorted_in[512:, :ROWS], "c", 1), in_own[:, ROWS:]], axis=1)
    with jax.named_scope("serve"):
        served, = call(serve_kernel, [((SHARDS * SLOTS, COLS), BF16)], asked, kv)
        near = exchange(served.reshape(SHARDS, SLOTS, COLS), NODES).reshape(SHARDS * SLOTS, COLS)
    with jax.named_scope("local"):
        sums, = call(
            local_kernel, [((ROWS, 4), F32)],
            edge_bias, query, from_left, kv, from_right, out_grad, virtual_kv, member, scalars=1,
        )
    with jax.named_scope("near"):
        send, stats, dnear = call(
            near_kernel, [((SHARDS * SLOTS, COLS), BF16), ((ROWS, 4), F32), ((ROWS, COLS), F32)],
            edge_bias, codes.T, codes.reshape(1, SLOTS * ROWS), query, near, out_grad, sums, scalars=1,
            scratch=[pltpu.VMEM((SLOTS * ROWS, COLS), BF16)],
        )
        back = exchange(send.reshape(SHARDS, SLOTS, COLS), NODES).reshape(SHARDS * SLOTS, COLS)
    with jax.named_scope("back"):
        dquery, dleft, down, dright, dvirtual = call(
            back_kernel,
            [((ROWS, COLS), BF16), ((ROWS, 2 * COLS), BF16), ((ROWS, 2 * COLS), F32), ((ROWS, 2 * COLS), BF16), ((VIRTUAL, 2 * COLS), F32)],
            edge_bias, query, from_left, kv, from_right, out_grad, virtual_kv, member, stats, dnear, scalars=1,
        )
        back_left = shift(dright, NODES, 1)
        back_right = shift(dleft, NODES, -1)
    with jax.named_scope("virtual"):
        split = jnp.concatenate(two_terms(dvirtual), axis=0)
        vnode = mul(split, flat_weight[:, COLS:], NT)
        vnode = vnode[:VIRTUAL] + vnode[VIRTUAL:]
        for bit in (1, 2):
            vnode = vnode + swap(vnode, "mp", bit)
        vnode = jnp.concatenate(two_terms(vnode.reshape(8, 512)), axis=0)
        tail = jnp.concatenate([jnp.pad(split, ((0, 8), (COLS, 0))), jnp.pad(vnode, ((0, 0), (0, COLS)))], axis=0)
    with jax.named_scope("total"):
        own, = call(
            total_kernel, [((ROWS + 32, 3 * COLS), BF16)],
            asked.reshape(1, SHARDS * SLOTS), back, dquery, down, back_left, back_right, tail,
        )
        other = swap(own, "c", 1)
    with jax.named_scope("feature"):
        partial = mul(own[:ROWS], flat_weight, NT).astype(BF16)
        me = lax.axis_index("mp")
        summed = lax.dynamic_slice_in_dim(partial, me * COLS, COLS, 1).astype(F32)
        for step in range(1, 4):
            piece = lax.dynamic_slice_in_dim(partial, ((me + step) % 4) * COLS, COLS, 1)
            summed = summed + shift(piece, "mp", step).astype(F32)
        feature_grad = summed.astype(BF16)
    with jax.named_scope("weight"):
        term, = call(weight_kernel, [((4, 144, 3 * COLS), BF16)], in_own, in_other, own, other, flops=3 * 10**8)
        term = jnp.sum(exchange(term, "x").astype(F32), axis=0)
        vnode = term[128:136, :512] + term[136:, :512]
        tail = jnp.broadcast_to(vnode[None], (16, 8, 512))
        term = jnp.concatenate([term[:128].reshape(16, 8, 3 * COLS), tail], axis=2).astype(BF16)
        term = jnp.sum(exchange(term, "z").astype(F32), axis=0)
        out_scale = 1.0 / math.sqrt(ROWS * SHARDS)
        weight_grad = (term[:, : 3 * COLS] * out_scale).reshape(8, 3, COLS)
        vnode_grad = (term[:, 3 * COLS :] * out_scale).reshape(VIRTUAL, width_in)
    return feature_grad, weight_grad, vnode_grad


def solution(mesh):
    fine = Mesh(mesh.devices.reshape(tuple(SIZES.values())), tuple(SIZES))
    return jax.shard_map(
        body,
        mesh=fine,
        in_specs=(
            P(NODES, None),
            P(None, None, "mp"),
            P(),
            P(None, "mp"),
            P(NODES, "mp"),
            P(None, NODES),
            P(NODES, None),
            P(NODES, None, None),
            P(NODES),
        ),
        out_specs=(P(NODES, "mp"), P(NODES, None, "mp"), P()),
        check_vma=False,
    )
```

```python
import math

import jax
import jax.numpy as jnp
from jax import lax
from jax.experimental import pallas as pl
from jax.experimental.pallas import tpu as pltpu
from jax.sharding import Mesh
from jax.sharding import PartitionSpec as P

HEAD = 128
TILE = 128
DEGREE = 4
VIRTUAL = 4
ROWS = 128
SHARDS = 128
COLS = 256
HEADS_DEV = 2
SLOTS = 2 * DEGREE
SIZES = {"z": 16, "x": 4, "c": 2, "mp": 4}
NODES = ("z", "x", "c")

SHARPNESS = 8.0
EPSILON = 1e-06
SCALE = SHARPNESS / HEAD
BOOST = math.log(TILE)
PRECISE = lax.Precision.HIGHEST
F32 = jnp.float32
BF16 = jnp.bfloat16

NN = (((1,), (0,)), ((), ()))
NT = (((1,), (1,)), ((), ()))
TN = (((0,), (0,)), ((), ()))


def mul(left, right, dims, precision=None):
    return lax.dot_general(left, right, dims, precision=precision, preferred_element_type=F32)


def unit(values):
    inv = lax.rsqrt(jnp.mean(values * values, axis=-1, keepdims=True) + EPSILON)
    return values * inv, inv


def unit_back(rows, inv, cotangent):
    return inv * (cotangent - rows * jnp.mean(rows * cotangent, axis=-1, keepdims=True))


def head_of(ref, head, part=0):
    start = part * COLS + head * HEAD
    return ref[:, start : start + HEAD]


def ones_where(condition):
    return jnp.where(condition, 1.0, 0.0).astype(BF16)


def shard_of(column):
    return lax.shift_right_logical(column, 7)


def ask_kernel(neighbours_ref, out_ref):
    shard = lax.broadcasted_iota(jnp.int32, (SHARDS, ROWS), 0)
    columns = []
    for perm in range(DEGREE):
        target = neighbours_ref[perm : perm + 1, :]
        rows = jnp.where(shard == shard_of(target), target & (ROWS - 1), 0)
        columns.append(jnp.sum(rows.astype(F32), axis=1, keepdims=True))
    out_ref[:, 0, :] = jnp.concatenate(columns, axis=1).astype(jnp.int32)


def slot(perm, part):
    return pl.ds(2 * perm + part, SHARDS, stride=SLOTS)


def take_slots(work_ref, perm):
    pieces = [work_ref[half, slot(perm, part), :] for part in range(2) for half in range(2)]
    return jnp.concatenate(pieces, axis=1).astype(BF16)


def put_slots(work_ref, perm, rows):
    for part in range(2):
        for half in range(2):
            at = part * COLS + half * HEAD
            work_ref[half, slot(perm, part), :] = rows[:, at : at + HEAD]


def open_slots(work_ref, rows_ref):
    for half in range(2):
        work_ref[half] = rows_ref[:, half * HEAD : (half + 1) * HEAD].astype(F32)


def close_slots(work_ref, rows_ref):
    for half in range(2):
        rows_ref[:, half * HEAD : (half + 1) * HEAD] = work_ref[half].astype(BF16)


def serve_kernel(asked_ref, kv_ref, out_ref, work_ref):
    row = lax.broadcasted_iota(jnp.int32, (SHARDS, ROWS), 1)
    asked, kv = asked_ref[:, 0, :], kv_ref[...]
    for perm in range(DEGREE):
        put_slots(work_ref, perm, mul(ones_where(row == asked[:, perm : perm + 1]), kv, NN))
    close_slots(work_ref, out_ref)


def virtual_weights(bias_ref, head, unit_q, virtual_ref, member_ref):
    unit_v, inv_v = unit(head_of(virtual_ref, head))
    scores = SCALE * mul(unit_q, unit_v, NT, PRECISE) + bias_ref[2, head] + BOOST
    return jnp.exp(scores) * member_ref[...].astype(F32), unit_v, inv_v


def turned(columns):
    wide = jnp.concatenate(columns + [jnp.zeros((ROWS, HEAD - len(columns)), F32)], axis=1)
    return wide.T[: len(columns)]


def local_kernel(bias_ref, query_ref, left_ref, own_ref, right_ref, grad_ref, virtual_ref, member_ref, sums_ref, query_out_ref, grad_out_ref):
    columns = []
    for head in range(HEADS_DEV):
        unit_q, _ = unit(head_of(query_ref, head))
        query = unit_q.astype(BF16)
        grad = head_of(grad_ref, head)
        total = jnp.zeros((ROWS, 1), F32)
        mixed = jnp.zeros((ROWS, 1), F32)
        for block in (left_ref, own_ref, right_ref):
            unit_k, _ = unit(head_of(block, head).astype(F32))
            weights = jnp.exp(SCALE * mul(query, unit_k.astype(BF16), NT) + bias_ref[0, head])
            grads = mul(grad, head_of(block, head, 1), NT)
            total += jnp.sum(weights, axis=1, keepdims=True)
            mixed += jnp.sum(weights * grads, axis=1, keepdims=True)
        weights, _, _ = virtual_weights(bias_ref, head, unit_q, virtual_ref, member_ref)
        grads = mul(grad.astype(F32), head_of(virtual_ref, head, 1), NT, PRECISE)
        total += jnp.sum(weights, axis=1, keepdims=True)
        mixed += jnp.sum(weights * grads, axis=1, keepdims=True)
        columns += [total, mixed]
        at = slice(head * HEAD, (head + 1) * HEAD)
        query_out_ref[at, :] = unit_q.T
        grad_out_ref[at, :] = grad.astype(F32).T
    sums_ref[...] = turned(columns)


def near_kernel(bias_ref, neighbours_ref, query_ref, near_ref, grad_ref, sums_ref, send_ref, stats_ref, dquery_ref, work_ref):
    totals = [sums_ref[2 * head : 2 * head + 1, :] for head in range(HEADS_DEV)]
    mixed = [sums_ref[2 * head + 1 : 2 * head + 2, :] for head in range(HEADS_DEV)]
    shard = lax.broadcasted_iota(jnp.int32, (SHARDS, ROWS), 0)
    hits = [ones_where(shard == shard_of(neighbours_ref[perm : perm + 1, :])) for perm in range(DEGREE)]
    unit_q = [query_ref[head * HEAD : (head + 1) * HEAD, :] for head in range(HEADS_DEV)]
    grad = [grad_ref[head * HEAD : (head + 1) * HEAD, :] for head in range(HEADS_DEV)]
    open_slots(work_ref, near_ref)
    saved = {}
    for perm in range(DEGREE):
        rows = mul(take_slots(work_ref, perm), hits[perm], TN)
        for head in range(HEADS_DEV):
            keys = rows[head * HEAD : (head + 1) * HEAD]
            values = rows[COLS + head * HEAD : COLS + (head + 1) * HEAD]
            inv_k = lax.rsqrt(jnp.mean(keys * keys, axis=0, keepdims=True) + EPSILON)
            unit_k = keys * inv_k
            product = jnp.sum(unit_q[head] * unit_k, axis=0, keepdims=True)
            weights = jnp.exp(SCALE * product + bias_ref[1, head] + BOOST)
            grads = jnp.sum(grad[head] * values, axis=0, keepdims=True)
            totals[head] = totals[head] + weights
            mixed[head] = mixed[head] + weights * grads
            saved[perm, head] = (unit_k, inv_k, product, weights, grads)
    inverse = [1.0 / total for total in totals]
    delta = [mixed[head] * inverse[head] for head in range(HEADS_DEV)]
    dquery = [jnp.zeros((HEAD, ROWS), F32) for _ in range(HEADS_DEV)]
    for perm in range(DEGREE):
        dkeys, dvalues = [], []
        for head in range(HEADS_DEV):
            unit_k, inv_k, product, weights, grads = saved[perm, head]
            probs = weights * inverse[head]
            dscores = probs * (grads - delta[head]) * SCALE
            dquery[head] = dquery[head] + dscores * unit_k
            factor = dscores * inv_k
            dkeys.append((factor * unit_q[head] - (factor * product * (1.0 / HEAD)) * unit_k).astype(BF16))
            dvalues.append((probs * grad[head]).astype(BF16))
        put_slots(work_ref, perm, mul(hits[perm], jnp.concatenate(dkeys + dvalues, axis=0), NT))
    close_slots(work_ref, send_ref)
    stats_ref[...] = jnp.concatenate([inverse[0], delta[0], inverse[1], delta[1]], axis=0)
    dquery_ref[...] = jnp.concatenate(dquery, axis=0)


def back_kernel(
    bias_ref, query_ref, left_ref, own_ref, right_ref, grad_ref, virtual_ref, member_ref, stats_ref, dnear_ref,
    dquery_ref, dleft_ref, down_ref, dright_ref, dvirtual_ref,
):
    stats = jnp.concatenate([stats_ref[...], jnp.zeros((HEAD - 2 * HEADS_DEV, ROWS), F32)], axis=0).T
    for head in range(HEADS_DEV):
        unit_q, inv_q = unit(head_of(query_ref, head))
        query = unit_q.astype(BF16)
        grad = head_of(grad_ref, head)
        inverse = stats[:, 2 * head : 2 * head + 1]
        delta = stats[:, 2 * head + 1 : 2 * head + 2]
        dquery = dnear_ref[head * HEAD : (head + 1) * HEAD, :].T
        keys_at = slice(head * HEAD, (head + 1) * HEAD)
        values_at = slice(COLS + head * HEAD, COLS + (head + 1) * HEAD)
        for block, out in ((left_ref, dleft_ref), (own_ref, down_ref), (right_ref, dright_ref)):
            unit_k, inv_k = unit(head_of(block, head).astype(F32))
            keys = unit_k.astype(BF16)
            probs = jnp.exp(SCALE * mul(query, keys, NT) + bias_ref[0, head]) * inverse
            grads = mul(grad, head_of(block, head, 1), NT)
            dscores = (probs * (grads - delta) * SCALE).astype(BF16)
            dquery += mul(dscores, keys, NN)
            out[:, keys_at] = unit_back(unit_k, inv_k, mul(dscores, query, TN)).astype(out.dtype)
            out[:, values_at] = mul(probs.astype(BF16), grad, TN).astype(out.dtype)
        weights, unit_v, inv_v = virtual_weights(bias_ref, head, unit_q, virtual_ref, member_ref)
        probs = weights * inverse
        wide = grad.astype(F32)
        grads = mul(wide, head_of(virtual_ref, head, 1), NT, PRECISE)
        dscores = probs * (grads - delta) * SCALE
        dquery += mul(dscores, unit_v, NN, PRECISE)
        dvirtual_ref[:, keys_at] = unit_back(unit_v, inv_v, mul(dscores, unit_q, TN, PRECISE))
        dvirtual_ref[:, values_at] = mul(probs, wide, TN, PRECISE)
        dquery_ref[:, keys_at] = unit_back(unit_q, inv_q, dquery).astype(BF16)


def total_kernel(asked_ref, back_ref, dquery_ref, down_ref, from_left_ref, from_right_ref, tail_ref, out_ref, work_ref):
    place = lax.broadcasted_iota(jnp.int32, (ROWS, SHARDS), 0)
    open_slots(work_ref, back_ref)
    rim = from_left_ref[...].astype(F32) + from_right_ref[...].astype(F32)
    total = down_ref[...] + rim
    for perm in range(DEGREE):
        total += mul(ones_where(place == asked_ref[perm : perm + 1, :]), take_slots(work_ref, perm), NN)
    out_ref[:ROWS, :COLS] = dquery_ref[...]
    out_ref[:ROWS, COLS:] = total.astype(BF16)
    out_ref[ROWS:, :] = tail_ref[...]


def weight_kernel(in_own_ref, in_other_ref, own_ref, other_ref, out_ref):
    own, other = own_ref[...], other_ref[...]
    vnode = own[ROWS + 16 :].astype(F32) + other[ROWS + 16 :].astype(F32)
    high, low = two_terms(vnode[:8] + vnode[8:])
    tail = jnp.concatenate([high.astype(F32), low.astype(F32)], axis=0).astype(BF16)
    for part in range(4):
        at = slice(part * 128, (part + 1) * 128)
        term = mul(in_own_ref[at, :], own, NN) + mul(in_other_ref[at, :], other, NN)
        out_ref[part, :128, :] = term.astype(BF16)
        out_ref[part, 128:, :] = tail


def finish_kernel(parts_ref, weight_ref, vnode_ref):
    out_scale = 1.0 / math.sqrt(ROWS * SHARDS)
    total = parts_ref[0].astype(F32)
    for part in range(1, SIZES["z"]):
        total += parts_ref[part].astype(F32)
    total *= out_scale
    for kind in range(3):
        weight_ref[kind] = total[:, kind * COLS : (kind + 1) * COLS]
    vnode_ref[:, :512] = total[:VIRTUAL, 3 * COLS :]
    vnode_ref[:, 512:] = total[VIRTUAL:, 3 * COLS :]


VMEM = pl.BlockSpec(memory_space=pltpu.VMEM)
SMEM = pl.BlockSpec(memory_space=pltpu.SMEM)
WORK = (pltpu.VMEM((2, SHARDS * SLOTS, HEAD), F32),)


def call(kernel, outs, *args, scalars=0, scratch=(), flops=10**8):
    shapes = [jax.ShapeDtypeStruct(shape, kind) for shape, kind in outs]
    moved = sum(math.prod(a.shape) * a.dtype.itemsize for a in [*args, *shapes])
    return pl.pallas_call(
        kernel,
        out_shape=shapes,
        in_specs=[SMEM] * scalars + [VMEM] * (len(args) - scalars),
        out_specs=[VMEM] * len(shapes),
        scratch_shapes=list(scratch),
        compiler_params=pltpu.CompilerParams(vmem_limit_bytes=32 * 2**20),
        cost_estimate=pl.CostEstimate(flops=flops, bytes_accessed=moved, transcendentals=0),
    )(*args)


def exchange(values, axis):
    return lax.all_to_all(values, axis, split_axis=0, concat_axis=0, tiled=True)


def shift(values, axis, step):
    count = math.prod(SIZES[name] for name in axis) if isinstance(axis, tuple) else SIZES[axis]
    return lax.ppermute(values, axis, [(i, (i + step) % count) for i in range(count)])


def swap(values, axis, bit):
    return lax.ppermute(values, axis, [(i, i ^ bit) for i in range(SIZES[axis])])


def two_terms(values):
    high = values.astype(BF16)
    return high, (values - high.astype(F32)).astype(BF16)


def body(features, qkv_weight, vnode_emb, edge_bias, out_grad, neighbours, member, tile_list, tile_count):
    width_in = qkv_weight.shape[0]
    with jax.named_scope("ask"):
        wanted, = call(ask_kernel, [((SHARDS, 1, DEGREE), jnp.int32)], neighbours)
        asked = exchange(wanted, NODES)
    with jax.named_scope("project"):
        flat_weight = qkv_weight.reshape(width_in, 3 * COLS)
        projected = jnp.dot(features, flat_weight, preferred_element_type=F32)
        query = projected[:, :COLS]
        kv = projected[:, COLS:].astype(BF16)
        virtual_kv = jnp.dot(vnode_emb, flat_weight[:, COLS:], preferred_element_type=F32)
        from_left = shift(kv, NODES, 1)
        from_right = shift(kv, NODES, -1)
    with jax.named_scope("select"):
        core = lax.axis_index("c")
        place = jnp.arange(width_in, dtype=jnp.int32)
        half, rest = place // 512, place % 512
        source = (rest // 8 % 16) * 64 + (rest // 128) * 16 + (half ^ core) * 8 + rest % 8
        chosen = (source[:, None] == jnp.arange(width_in, dtype=jnp.int32)[None, :]).astype(BF16)
        rows_in = jnp.concatenate([features, vnode_emb, vnode_emb, jnp.zeros((24, width_in), BF16)], axis=0)
        sorted_in = mul(chosen, rows_in, NT).astype(BF16)
        in_own = sorted_in[:512]
        in_other = jnp.concatenate([swap(sorted_in[512:, :ROWS], "c", 1), in_own[:, ROWS:]], axis=1)
    with jax.named_scope("serve"):
        served, = call(serve_kernel, [((SHARDS * SLOTS, COLS), BF16)], asked, kv, scratch=WORK)
        near = exchange(served.reshape(SHARDS, SLOTS, COLS), NODES).reshape(SHARDS * SLOTS, COLS)
    with jax.named_scope("local"):
        sums, query_turned, grad_turned = call(
            local_kernel, [((2 * HEADS_DEV, ROWS), F32), ((COLS, ROWS), F32), ((COLS, ROWS), F32)],
            edge_bias, query, from_left, kv, from_right, out_grad, virtual_kv, member, scalars=1,
        )
    with jax.named_scope("near"):
        send, stats, dnear = call(
            near_kernel, [((SHARDS * SLOTS, COLS), BF16), ((2 * HEADS_DEV, ROWS), F32), ((COLS, ROWS), F32)],
            edge_bias, neighbours, query_turned, near, grad_turned, sums, scalars=1, scratch=WORK,
        )
        back = exchange(send.reshape(SHARDS, SLOTS, COLS), NODES).reshape(SHARDS * SLOTS, COLS)
    with jax.named_scope("back"):
        dquery, dleft, down, dright, dvirtual = call(
            back_kernel,
            [((ROWS, COLS), BF16), ((ROWS, 2 * COLS), BF16), ((ROWS, 2 * COLS), F32), ((ROWS, 2 * COLS), BF16), ((VIRTUAL, 2 * COLS), F32)],
            edge_bias, query, from_left, kv, from_right, out_grad, virtual_kv, member, stats, dnear, scalars=1,
        )
        back_left = shift(dright, NODES, 1)
        back_right = shift(dleft, NODES, -1)
    with jax.named_scope("virtual"):
        split = jnp.concatenate(two_terms(dvirtual), axis=0)
        vnode = mul(split, flat_weight[:, COLS:], NT)
        vnode = vnode[:VIRTUAL] + vnode[VIRTUAL:]
        for bit in (1, 2):
            vnode = vnode + swap(vnode, "mp", bit)
        vnode = jnp.concatenate(two_terms(jnp.concatenate([vnode[:, :512], vnode[:, 512:]], axis=0)), axis=0)
        tail = jnp.concatenate([jnp.pad(split, ((0, 8), (COLS, 0))), jnp.pad(vnode, ((0, 0), (0, COLS)))], axis=0)
    with jax.named_scope("total"):
        own, = call(
            total_kernel, [((ROWS + 32, 3 * COLS), BF16)],
            asked.reshape(SHARDS, DEGREE).T, back, dquery, down, back_left, back_right, tail, scratch=WORK,
        )
        other = swap(own, "c", 1)
    with jax.named_scope("feature"):
        partial = mul(own[:ROWS], flat_weight, NT).astype(BF16)
        me = lax.axis_index("mp")
        summed = lax.dynamic_slice_in_dim(partial, me * COLS, COLS, 1).astype(F32)
        for step in range(1, 4):
            piece = lax.dynamic_slice_in_dim(partial, ((me + step) % 4) * COLS, COLS, 1)
            summed = summed + shift(piece, "mp", step).astype(F32)
        feature_grad = summed.astype(BF16)
    with jax.named_scope("weight"):
        term, = call(weight_kernel, [((4, 144, 3 * COLS), BF16)], in_own, in_other, own, other, flops=3 * 10**8)
        term = jnp.sum(exchange(term, "x").astype(F32), axis=0)
        vnode = term[128:136, :512] + term[136:, :512]
        tail = jnp.broadcast_to(vnode[None], (16, 8, 512))
        term = jnp.concatenate([term[:128].reshape(16, 8, 3 * COLS), tail], axis=2).astype(BF16)
        weight_grad, vnode_grad = call(
            finish_kernel, [((3, 8, COLS), F32), ((VIRTUAL, width_in), F32)], exchange(term, "z"),
        )
        weight_grad = weight_grad.transpose(1, 0, 2)
    return feature_grad, weight_grad, vnode_grad


def solution(mesh):
    fine = Mesh(mesh.devices.reshape(tuple(SIZES.values())), tuple(SIZES))
    return jax.shard_map(
        body,
        mesh=fine,
        in_specs=(
            P(NODES, None),
            P(None, None, "mp"),
            P(),
            P(None, "mp"),
            P(NODES, "mp"),
            P(None, NODES),
            P(NODES, None),
            P(NODES, None, None),
            P(NODES),
        ),
        out_specs=(P(NODES, "mp"), P(NODES, None, "mp"), P()),
        check_vma=False,
    )
```

```python
import math

import jax
import jax.numpy as jnp
from jax import lax
from jax.experimental import pallas as pl
from jax.experimental.pallas import tpu as pltpu
from jax.sharding import Mesh
from jax.sharding import PartitionSpec as P

HEAD = 128
TILE = 128
DEGREE = 4
VIRTUAL = 4
ROWS = 128
SHARDS = 128
COLS = 256
HEADS_DEV = 2
SLOTS = 2 * DEGREE
SIZES = {"z": 16, "x": 4, "c": 2, "mp": 4}
NODES = ("z", "x", "c")

SHARPNESS = 8.0
EPSILON = 1e-06
SCALE = SHARPNESS / HEAD
BOOST = math.log(TILE)
PRECISE = lax.Precision.HIGHEST
F32 = jnp.float32
BF16 = jnp.bfloat16

NN = (((1,), (0,)), ((), ()))
NT = (((1,), (1,)), ((), ()))
TN = (((0,), (0,)), ((), ()))


def mul(left, right, dims, precision=None):
    return lax.dot_general(left, right, dims, precision=precision, preferred_element_type=F32)


def unit(values):
    inv = lax.rsqrt(jnp.mean(values * values, axis=-1, keepdims=True) + EPSILON)
    return values * inv, inv


def unit_back(rows, inv, cotangent):
    return inv * (cotangent - rows * jnp.mean(rows * cotangent, axis=-1, keepdims=True))


def head_of(ref, head, part=0):
    start = part * COLS + head * HEAD
    return ref[:, start : start + HEAD]


def ones_where(condition):
    return jnp.where(condition, 1.0, 0.0).astype(BF16)


def shard_of(column):
    return lax.shift_right_logical(column, 7)


def ask_kernel(neighbours_ref, out_ref):
    shard = lax.broadcasted_iota(jnp.int32, (SHARDS, ROWS), 0)
    columns = []
    for perm in range(DEGREE):
        target = neighbours_ref[perm : perm + 1, :]
        rows = jnp.where(shard == shard_of(target), target & (ROWS - 1), 0)
        columns.append(jnp.sum(rows.astype(F32), axis=1, keepdims=True))
    out_ref[:, 0, :] = jnp.concatenate(columns, axis=1).astype(jnp.int32)


def slot(perm, part):
    return pl.ds(2 * perm + part, SHARDS, stride=SLOTS)


def take_slots(work_ref, perm):
    pieces = [work_ref[half, slot(perm, part), :] for part in range(2) for half in range(2)]
    return jnp.concatenate(pieces, axis=1).astype(BF16)


def put_slots(work_ref, perm, rows):
    for part in range(2):
        for half in range(2):
            at = part * COLS + half * HEAD
            work_ref[half, slot(perm, part), :] = rows[:, at : at + HEAD]


def open_slots(work_ref, rows_ref):
    for half in range(2):
        work_ref[half] = rows_ref[:, half * HEAD : (half + 1) * HEAD].astype(F32)


def close_slots(work_ref, rows_ref):
    for half in range(2):
        rows_ref[:, half * HEAD : (half + 1) * HEAD] = work_ref[half].astype(BF16)


def serve_kernel(asked_ref, kv_ref, out_ref, work_ref):
    row = lax.broadcasted_iota(jnp.int32, (SHARDS, ROWS), 1)
    asked, kv = asked_ref[:, 0, :], kv_ref[...]
    for perm in range(DEGREE):
        put_slots(work_ref, perm, mul(ones_where(row == asked[:, perm : perm + 1]), kv, NN))
    close_slots(work_ref, out_ref)


def virtual_weights(bias_ref, head, unit_q, virtual_ref, member_ref):
    unit_v, inv_v = unit(head_of(virtual_ref, head))
    scores = SCALE * mul(unit_q, unit_v, NT, PRECISE) + bias_ref[2, head] + BOOST
    return jnp.exp(scores) * member_ref[...].astype(F32), unit_v, inv_v


def turned(columns):
    wide = jnp.concatenate(columns + [jnp.zeros((ROWS, HEAD - len(columns)), F32)], axis=1)
    return wide.T[: len(columns)]


def local_kernel(bias_ref, query_ref, left_ref, own_ref, right_ref, grad_ref, virtual_ref, member_ref, sums_ref, query_out_ref, grad_out_ref):
    columns = []
    for head in range(HEADS_DEV):
        unit_q, _ = unit(head_of(query_ref, head))
        query = unit_q.astype(BF16)
        grad = head_of(grad_ref, head)
        total = jnp.zeros((ROWS, 1), F32)
        mixed = jnp.zeros((ROWS, 1), F32)
        for block in (left_ref, own_ref, right_ref):
            unit_k, _ = unit(head_of(block, head).astype(F32))
            weights = jnp.exp(SCALE * mul(query, unit_k.astype(BF16), NT) + bias_ref[0, head])
            grads = mul(grad, head_of(block, head, 1), NT)
            total += jnp.sum(weights, axis=1, keepdims=True)
            mixed += jnp.sum(weights * grads, axis=1, keepdims=True)
        weights, _, _ = virtual_weights(bias_ref, head, unit_q, virtual_ref, member_ref)
        grads = mul(grad.astype(F32), head_of(virtual_ref, head, 1), NT, PRECISE)
        total += jnp.sum(weights, axis=1, keepdims=True)
        mixed += jnp.sum(weights * grads, axis=1, keepdims=True)
        columns += [total, mixed]
        at = slice(head * HEAD, (head + 1) * HEAD)
        query_out_ref[at, :] = unit_q.T
        grad_out_ref[at, :] = grad.astype(F32).T
    sums_ref[...] = turned(columns)


def near_kernel(bias_ref, neighbours_ref, query_ref, near_ref, grad_ref, sums_ref, send_ref, stats_ref, dquery_ref, work_ref):
    totals = [sums_ref[2 * head : 2 * head + 1, :] for head in range(HEADS_DEV)]
    mixed = [sums_ref[2 * head + 1 : 2 * head + 2, :] for head in range(HEADS_DEV)]
    shard = lax.broadcasted_iota(jnp.int32, (SHARDS, ROWS), 0)
    hits = [ones_where(shard == shard_of(neighbours_ref[perm : perm + 1, :])) for perm in range(DEGREE)]
    unit_q = [query_ref[head * HEAD : (head + 1) * HEAD, :] for head in range(HEADS_DEV)]
    grad = [grad_ref[head * HEAD : (head + 1) * HEAD, :] for head in range(HEADS_DEV)]
    open_slots(work_ref, near_ref)
    saved = {}
    for perm in range(DEGREE):
        rows = mul(take_slots(work_ref, perm), hits[perm], TN)
        for head in range(HEADS_DEV):
            keys = rows[head * HEAD : (head + 1) * HEAD]
            values = rows[COLS + head * HEAD : COLS + (head + 1) * HEAD]
            inv_k = lax.rsqrt(jnp.mean(keys * keys, axis=0, keepdims=True) + EPSILON)
            unit_k = keys * inv_k
            product = jnp.sum(unit_q[head] * unit_k, axis=0, keepdims=True)
            weights = jnp.exp(SCALE * product + bias_ref[1, head] + BOOST)
            grads = jnp.sum(grad[head] * values, axis=0, keepdims=True)
            totals[head] = totals[head] + weights
            mixed[head] = mixed[head] + weights * grads
            saved[perm, head] = (unit_k, inv_k, product, weights, grads)
    inverse = [1.0 / total for total in totals]
    delta = [mixed[head] * inverse[head] for head in range(HEADS_DEV)]
    dquery = [jnp.zeros((HEAD, ROWS), F32) for _ in range(HEADS_DEV)]
    for perm in range(DEGREE):
        dkeys, dvalues = [], []
        for head in range(HEADS_DEV):
            unit_k, inv_k, product, weights, grads = saved[perm, head]
            probs = weights * inverse[head]
            dscores = probs * (grads - delta[head]) * SCALE
            dquery[head] = dquery[head] + dscores * unit_k
            factor = dscores * inv_k
            dkeys.append((factor * unit_q[head] - (factor * product * (1.0 / HEAD)) * unit_k).astype(BF16))
            dvalues.append((probs * grad[head]).astype(BF16))
        put_slots(work_ref, perm, mul(hits[perm], jnp.concatenate(dkeys + dvalues, axis=0), NT))
    close_slots(work_ref, send_ref)
    stats_ref[...] = jnp.concatenate([inverse[0], delta[0], inverse[1], delta[1]], axis=0)
    dquery_ref[...] = jnp.concatenate(dquery, axis=0)


def back_kernel(
    bias_ref, query_ref, left_ref, own_ref, right_ref, grad_ref, virtual_ref, member_ref, stats_ref, dnear_ref,
    dquery_ref, dleft_ref, down_ref, dright_ref, dvirtual_ref,
):
    stats = jnp.concatenate([stats_ref[...], jnp.zeros((HEAD - 2 * HEADS_DEV, ROWS), F32)], axis=0).T
    for head in range(HEADS_DEV):
        unit_q, inv_q = unit(head_of(query_ref, head))
        query = unit_q.astype(BF16)
        grad = head_of(grad_ref, head)
        inverse = stats[:, 2 * head : 2 * head + 1]
        delta = stats[:, 2 * head + 1 : 2 * head + 2]
        dquery = dnear_ref[head * HEAD : (head + 1) * HEAD, :].T
        keys_at = slice(head * HEAD, (head + 1) * HEAD)
        values_at = slice(COLS + head * HEAD, COLS + (head + 1) * HEAD)
        for block, out in ((left_ref, dleft_ref), (own_ref, down_ref), (right_ref, dright_ref)):
            unit_k, inv_k = unit(head_of(block, head).astype(F32))
            keys = unit_k.astype(BF16)
            probs = jnp.exp(SCALE * mul(query, keys, NT) + bias_ref[0, head]) * inverse
            grads = mul(grad, head_of(block, head, 1), NT)
            dscores = (probs * (grads - delta) * SCALE).astype(BF16)
            dquery += mul(dscores, keys, NN)
            out[:, keys_at] = unit_back(unit_k, inv_k, mul(dscores, query, TN)).astype(out.dtype)
            out[:, values_at] = mul(probs.astype(BF16), grad, TN).astype(out.dtype)
        weights, unit_v, inv_v = virtual_weights(bias_ref, head, unit_q, virtual_ref, member_ref)
        probs = weights * inverse
        wide = grad.astype(F32)
        grads = mul(wide, head_of(virtual_ref, head, 1), NT, PRECISE)
        dscores = probs * (grads - delta) * SCALE
        dquery += mul(dscores, unit_v, NN, PRECISE)
        dvirtual_ref[:, keys_at] = unit_back(unit_v, inv_v, mul(dscores, unit_q, TN, PRECISE))
        dvirtual_ref[:, values_at] = mul(probs, wide, TN, PRECISE)
        dquery_ref[:, keys_at] = unit_back(unit_q, inv_q, dquery).astype(BF16)


def total_kernel(asked_ref, back_ref, dquery_ref, down_ref, from_left_ref, from_right_ref, tail_ref, out_ref, work_ref):
    place = lax.broadcasted_iota(jnp.int32, (ROWS, SHARDS), 0)
    open_slots(work_ref, back_ref)
    rim = from_left_ref[...].astype(F32) + from_right_ref[...].astype(F32)
    total = down_ref[...] + rim
    for perm in range(DEGREE):
        total += mul(ones_where(place == asked_ref[perm : perm + 1, :]), take_slots(work_ref, perm), NN)
    out_ref[:ROWS, :COLS] = dquery_ref[...]
    out_ref[:ROWS, COLS:] = total.astype(BF16)
    out_ref[ROWS:, :] = tail_ref[...]


def weight_kernel(in_own_ref, in_other_ref, own_ref, other_ref, out_ref):
    own, other = own_ref[...], other_ref[...]
    vnode = own[ROWS + 16 :].astype(F32) + other[ROWS + 16 :].astype(F32)
    vnode = vnode[:8] + vnode[8:]
    for part in range(4):
        at = slice(part * 128, (part + 1) * 128)
        term = mul(in_own_ref[at, :], own, NN) + mul(in_other_ref[at, :], other, NN)
        out_ref[part] = jnp.concatenate([term, vnode], axis=0).astype(BF16)


def finish_kernel(parts_ref, weight_ref, vnode_ref):
    out_scale = 1.0 / math.sqrt(ROWS * SHARDS)
    total = parts_ref[0].astype(F32)
    for part in range(1, SIZES["z"]):
        total += parts_ref[part].astype(F32)
    total *= out_scale
    for kind in range(3):
        weight_ref[kind] = total[:, kind * COLS : (kind + 1) * COLS]
    vnode_ref[:, :512] = total[:VIRTUAL, 3 * COLS :]
    vnode_ref[:, 512:] = total[VIRTUAL:, 3 * COLS :]


VMEM = pl.BlockSpec(memory_space=pltpu.VMEM)
SMEM = pl.BlockSpec(memory_space=pltpu.SMEM)
WORK = (pltpu.VMEM((2, SHARDS * SLOTS, HEAD), F32),)


def call(kernel, outs, *args, scalars=0, scratch=(), flops=10**8):
    shapes = [jax.ShapeDtypeStruct(shape, kind) for shape, kind in outs]
    moved = sum(math.prod(a.shape) * a.dtype.itemsize for a in [*args, *shapes])
    return pl.pallas_call(
        kernel,
        out_shape=shapes,
        in_specs=[SMEM] * scalars + [VMEM] * (len(args) - scalars),
        out_specs=[VMEM] * len(shapes),
        scratch_shapes=list(scratch),
        compiler_params=pltpu.CompilerParams(vmem_limit_bytes=32 * 2**20),
        cost_estimate=pl.CostEstimate(flops=flops, bytes_accessed=moved, transcendentals=0),
    )(*args)


def exchange(values, axis):
    return lax.all_to_all(values, axis, split_axis=0, concat_axis=0, tiled=True)


def shift(values, axis, step):
    count = math.prod(SIZES[name] for name in axis) if isinstance(axis, tuple) else SIZES[axis]
    return lax.ppermute(values, axis, [(i, (i + step) % count) for i in range(count)])


def swap(values, axis, bit):
    return lax.ppermute(values, axis, [(i, i ^ bit) for i in range(SIZES[axis])])


def sum_of_four(values, axis):
    near, far, both = (swap(values, axis, bit) for bit in (1, 2, 3))
    return (values + near) + (far + both)


def two_terms(values):
    high = values.astype(BF16)
    return high, (values - high.astype(F32)).astype(BF16)


def body(features, qkv_weight, vnode_emb, edge_bias, out_grad, neighbours, member, tile_list, tile_count):
    width_in = qkv_weight.shape[0]
    with jax.named_scope("ask"):
        wanted, = call(ask_kernel, [((SHARDS, 1, DEGREE), jnp.int32)], neighbours)
        asked = exchange(wanted, NODES)
    with jax.named_scope("project"):
        flat_weight = qkv_weight.reshape(width_in, 3 * COLS)
        projected = jnp.dot(features, flat_weight, preferred_element_type=F32)
        query = projected[:, :COLS]
        kv = projected[:, COLS:].astype(BF16)
        virtual_kv = jnp.dot(vnode_emb, flat_weight[:, COLS:], preferred_element_type=F32)
        from_left = shift(kv, NODES, 1)
        from_right = shift(kv, NODES, -1)
    with jax.named_scope("select"):
        core = lax.axis_index("c")
        place = jnp.arange(width_in, dtype=jnp.int32)
        half, rest = place // 512, place % 512
        source = (rest // 8 % 16) * 64 + (rest // 128) * 16 + (half ^ core) * 8 + rest % 8
        chosen = (source[:, None] == jnp.arange(width_in, dtype=jnp.int32)[None, :]).astype(BF16)
        rows_in = jnp.concatenate([features, vnode_emb, vnode_emb, jnp.zeros((24, width_in), BF16)], axis=0)
        sorted_in = mul(chosen, rows_in, NT).astype(BF16)
        in_own = sorted_in[:512]
        in_other = jnp.concatenate([swap(sorted_in[512:, :ROWS], "c", 1), in_own[:, ROWS:]], axis=1)
        from_left, from_right, in_own, in_other = lax.optimization_barrier((from_left, from_right, in_own, in_other))
    with jax.named_scope("serve"):
        served, = call(serve_kernel, [((SHARDS * SLOTS, COLS), BF16)], asked, kv, scratch=WORK)
        near = exchange(served.reshape(SHARDS, SLOTS, COLS), NODES).reshape(SHARDS * SLOTS, COLS)
    with jax.named_scope("local"):
        sums, query_turned, grad_turned = call(
            local_kernel, [((2 * HEADS_DEV, ROWS), F32), ((COLS, ROWS), F32), ((COLS, ROWS), F32)],
            edge_bias, query, from_left, kv, from_right, out_grad, virtual_kv, member, scalars=1,
        )
    with jax.named_scope("near"):
        send, stats, dnear = call(
            near_kernel, [((SHARDS * SLOTS, COLS), BF16), ((2 * HEADS_DEV, ROWS), F32), ((COLS, ROWS), F32)],
            edge_bias, neighbours, query_turned, near, grad_turned, sums, scalars=1, scratch=WORK,
        )
        back = exchange(send.reshape(SHARDS, SLOTS, COLS), NODES).reshape(SHARDS * SLOTS, COLS)
    with jax.named_scope("back"):
        dquery, dleft, down, dright, dvirtual = call(
            back_kernel,
            [((ROWS, COLS), BF16), ((ROWS, 2 * COLS), BF16), ((ROWS, 2 * COLS), F32), ((ROWS, 2 * COLS), BF16), ((VIRTUAL, 2 * COLS), F32)],
            edge_bias, query, from_left, kv, from_right, out_grad, virtual_kv, member, stats, dnear, scalars=1,
        )
        back_left = shift(dright, NODES, 1)
        back_right = shift(dleft, NODES, -1)
    with jax.named_scope("virtual"):
        split = jnp.concatenate(two_terms(dvirtual), axis=0)
        vnode = mul(split, flat_weight[:, COLS:], NT)
        vnode = vnode[:VIRTUAL] + vnode[VIRTUAL:]
        vnode = sum_of_four(vnode, "mp")
        vnode = jnp.concatenate(two_terms(jnp.concatenate([vnode[:, :512], vnode[:, 512:]], axis=0)), axis=0)
        tail = jnp.concatenate([jnp.pad(split, ((0, 8), (COLS, 0))), jnp.pad(vnode, ((0, 0), (0, COLS)))], axis=0)
    with jax.named_scope("total"):
        own, = call(
            total_kernel, [((ROWS + 32, 3 * COLS), BF16)],
            asked.reshape(SHARDS, DEGREE).T, back, dquery, down, back_left, back_right, tail, scratch=WORK,
        )
        other = swap(own, "c", 1)
    with jax.named_scope("feature"):
        partial = mul(own[:ROWS], flat_weight, NT).astype(BF16)
        me = lax.axis_index("mp")
        summed = lax.dynamic_slice_in_dim(partial, me * COLS, COLS, 1).astype(F32)
        for step in range(1, 4):
            piece = lax.dynamic_slice_in_dim(partial, ((me + step) % 4) * COLS, COLS, 1)
            summed = summed + shift(piece, "mp", step).astype(F32)
        feature_grad = summed.astype(BF16)
    with jax.named_scope("weight"):
        term, = call(weight_kernel, [((4, 136, 3 * COLS), BF16)], in_own, in_other, own, other, flops=3 * 10**8)
        term = jnp.sum(exchange(term, "x").astype(F32), axis=0)
        vnode = term[128:, :512]
        tail = jnp.broadcast_to(vnode[None], (16, 8, 512))
        term = jnp.concatenate([term[:128].reshape(16, 8, 3 * COLS), tail], axis=2).astype(BF16)
        weight_grad, vnode_grad = call(
            finish_kernel, [((3, 8, COLS), F32), ((VIRTUAL, width_in), F32)], exchange(term, "z"),
        )
        weight_grad = weight_grad.transpose(1, 0, 2)
    return feature_grad, weight_grad, vnode_grad


def solution(mesh):
    fine = Mesh(mesh.devices.reshape(tuple(SIZES.values())), tuple(SIZES))
    return jax.shard_map(
        body,
        mesh=fine,
        in_specs=(
            P(NODES, None),
            P(None, None, "mp"),
            P(),
            P(None, "mp"),
            P(NODES, "mp"),
            P(None, NODES),
            P(NODES, None),
            P(NODES, None, None),
            P(NODES),
        ),
        out_specs=(P(NODES, "mp"), P(NODES, None, "mp"), P()),
        check_vma=False,
    )
```

```python
import math

import jax
import jax.numpy as jnp
from jax import lax
from jax.experimental import pallas as pl
from jax.experimental.pallas import tpu as pltpu
from jax.sharding import Mesh
from jax.sharding import PartitionSpec as P

HEAD = 128
TILE = 128
DEGREE = 4
VIRTUAL = 4
ROWS = 128
SHARDS = 128
COLS = 256
HEADS_DEV = 2
SLOTS = 2 * DEGREE
SIZES = {"z": 16, "x": 4, "c": 2, "mp": 4}
NODES = ("z", "x", "c")

SHARPNESS = 8.0
EPSILON = 1e-06
SCALE = SHARPNESS / HEAD
BOOST = math.log(TILE)
PRECISE = lax.Precision.HIGHEST
F32 = jnp.float32
BF16 = jnp.bfloat16

NN = (((1,), (0,)), ((), ()))
NT = (((1,), (1,)), ((), ()))
TN = (((0,), (0,)), ((), ()))


def mul(left, right, dims, precision=None):
    return lax.dot_general(left, right, dims, precision=precision, preferred_element_type=F32)


def unit(values):
    inv = lax.rsqrt(jnp.mean(values * values, axis=-1, keepdims=True) + EPSILON)
    return values * inv, inv


def unit_back(rows, inv, cotangent):
    return inv * (cotangent - rows * jnp.mean(rows * cotangent, axis=-1, keepdims=True))


def head_of(ref, head, part=0):
    start = part * COLS + head * HEAD
    return ref[:, start : start + HEAD]


def ones_where(condition):
    return jnp.where(condition, 1.0, 0.0).astype(BF16)


def shard_of(column):
    return lax.shift_right_logical(column, 7)


def ask_kernel(neighbours_ref, out_ref):
    shard = lax.broadcasted_iota(jnp.int32, (SHARDS, ROWS), 0)
    columns = []
    for perm in range(DEGREE):
        target = neighbours_ref[perm : perm + 1, :]
        rows = jnp.where(shard == shard_of(target), target & (ROWS - 1), 0)
        columns.append(jnp.sum(rows.astype(F32), axis=1, keepdims=True))
    out_ref[:, 0, :] = jnp.concatenate(columns, axis=1).astype(jnp.int32)


def slot(perm, part):
    return pl.ds(2 * perm + part, SHARDS, stride=SLOTS)


def take_slots(work_ref, perm):
    pieces = [work_ref[half, slot(perm, part), :] for part in range(2) for half in range(2)]
    return jnp.concatenate(pieces, axis=1).astype(BF16)


def put_slots(work_ref, perm, rows):
    for part in range(2):
        for half in range(2):
            at = part * COLS + half * HEAD
            work_ref[half, slot(perm, part), :] = rows[:, at : at + HEAD]


def open_slots(work_ref, rows_ref):
    for half in range(2):
        work_ref[half] = rows_ref[:, half * HEAD : (half + 1) * HEAD].astype(F32)


def close_slots(work_ref, rows_ref):
    for half in range(2):
        rows_ref[:, half * HEAD : (half + 1) * HEAD] = work_ref[half].astype(BF16)


def serve_kernel(asked_ref, kv_ref, out_ref, work_ref):
    row = lax.broadcasted_iota(jnp.int32, (SHARDS, ROWS), 1)
    asked = asked_ref[:, 0, :]
    hits = jnp.concatenate([ones_where(row == asked[:, perm : perm + 1]) for perm in range(DEGREE)], axis=0)
    picked = mul(hits, kv_ref[...], NN)
    for perm in range(DEGREE):
        put_slots(work_ref, perm, picked[perm * SHARDS : (perm + 1) * SHARDS])
    close_slots(work_ref, out_ref)


def virtual_weights(bias_ref, head, unit_q, virtual_ref, member_ref):
    unit_v, inv_v = unit(head_of(virtual_ref, head))
    scores = SCALE * mul(unit_q, unit_v, NT, PRECISE) + bias_ref[2, head] + BOOST
    return jnp.exp(scores) * member_ref[...].astype(F32), unit_v, inv_v


def turned(columns):
    wide = jnp.concatenate(columns + [jnp.zeros((ROWS, HEAD - len(columns)), F32)], axis=1)
    return wide.T[: len(columns)]


def local_kernel(bias_ref, query_ref, left_ref, own_ref, right_ref, grad_ref, virtual_ref, member_ref, sums_ref, query_out_ref, grad_out_ref):
    columns = []
    for head in range(HEADS_DEV):
        unit_q, _ = unit(head_of(query_ref, head))
        query = unit_q.astype(BF16)
        grad = head_of(grad_ref, head)
        total = jnp.zeros((ROWS, 1), F32)
        mixed = jnp.zeros((ROWS, 1), F32)
        for block in (left_ref, own_ref, right_ref):
            unit_k, _ = unit(head_of(block, head).astype(F32))
            weights = jnp.exp(SCALE * mul(query, unit_k.astype(BF16), NT) + bias_ref[0, head])
            grads = mul(grad, head_of(block, head, 1), NT)
            total += jnp.sum(weights, axis=1, keepdims=True)
            mixed += jnp.sum(weights * grads, axis=1, keepdims=True)
        weights, _, _ = virtual_weights(bias_ref, head, unit_q, virtual_ref, member_ref)
        grads = mul(grad.astype(F32), head_of(virtual_ref, head, 1), NT, PRECISE)
        total += jnp.sum(weights, axis=1, keepdims=True)
        mixed += jnp.sum(weights * grads, axis=1, keepdims=True)
        columns += [total, mixed]
        at = slice(head * HEAD, (head + 1) * HEAD)
        query_out_ref[at, :] = unit_q.T
        grad_out_ref[at, :] = grad.astype(F32).T
    sums_ref[...] = turned(columns)


def near_kernel(bias_ref, neighbours_ref, query_ref, near_ref, grad_ref, sums_ref, send_ref, stats_ref, dquery_ref, work_ref):
    totals = [sums_ref[2 * head : 2 * head + 1, :] for head in range(HEADS_DEV)]
    mixed = [sums_ref[2 * head + 1 : 2 * head + 2, :] for head in range(HEADS_DEV)]
    shard = lax.broadcasted_iota(jnp.int32, (SHARDS, ROWS), 0)
    hits = [ones_where(shard == shard_of(neighbours_ref[perm : perm + 1, :])) for perm in range(DEGREE)]
    unit_q = [query_ref[head * HEAD : (head + 1) * HEAD, :] for head in range(HEADS_DEV)]
    grad = [grad_ref[head * HEAD : (head + 1) * HEAD, :] for head in range(HEADS_DEV)]
    open_slots(work_ref, near_ref)
    saved = {}
    for perm in range(DEGREE):
        rows = mul(take_slots(work_ref, perm), hits[perm], TN)
        for head in range(HEADS_DEV):
            keys = rows[head * HEAD : (head + 1) * HEAD]
            values = rows[COLS + head * HEAD : COLS + (head + 1) * HEAD]
            inv_k = lax.rsqrt(jnp.mean(keys * keys, axis=0, keepdims=True) + EPSILON)
            unit_k = keys * inv_k
            product = jnp.sum(unit_q[head] * unit_k, axis=0, keepdims=True)
            weights = jnp.exp(SCALE * product + bias_ref[1, head] + BOOST)
            grads = jnp.sum(grad[head] * values, axis=0, keepdims=True)
            totals[head] = totals[head] + weights
            mixed[head] = mixed[head] + weights * grads
            saved[perm, head] = (unit_k, inv_k, product, weights, grads)
    inverse = [1.0 / total for total in totals]
    delta = [mixed[head] * inverse[head] for head in range(HEADS_DEV)]
    dquery = [jnp.zeros((HEAD, ROWS), F32) for _ in range(HEADS_DEV)]
    for perm in range(DEGREE):
        dkeys, dvalues = [], []
        for head in range(HEADS_DEV):
            unit_k, inv_k, product, weights, grads = saved[perm, head]
            probs = weights * inverse[head]
            dscores = probs * (grads - delta[head]) * SCALE
            dquery[head] = dquery[head] + dscores * unit_k
            factor = dscores * inv_k
            dkeys.append((factor * unit_q[head] - (factor * product * (1.0 / HEAD)) * unit_k).astype(BF16))
            dvalues.append((probs * grad[head]).astype(BF16))
        put_slots(work_ref, perm, mul(hits[perm], jnp.concatenate(dkeys + dvalues, axis=0), NT))
    close_slots(work_ref, send_ref)
    stats_ref[...] = jnp.concatenate([inverse[0], delta[0], inverse[1], delta[1]], axis=0)
    dquery_ref[...] = jnp.concatenate(dquery, axis=0)


def back_kernel(
    bias_ref, query_ref, left_ref, own_ref, right_ref, grad_ref, virtual_ref, member_ref, stats_ref, dnear_ref,
    dquery_ref, dleft_ref, down_ref, dright_ref, dvirtual_ref,
):
    stats = jnp.concatenate([stats_ref[...], jnp.zeros((HEAD - 2 * HEADS_DEV, ROWS), F32)], axis=0).T
    for head in range(HEADS_DEV):
        unit_q, inv_q = unit(head_of(query_ref, head))
        query = unit_q.astype(BF16)
        grad = head_of(grad_ref, head)
        inverse = stats[:, 2 * head : 2 * head + 1]
        delta = stats[:, 2 * head + 1 : 2 * head + 2]
        dquery = dnear_ref[head * HEAD : (head + 1) * HEAD, :].T
        keys_at = slice(head * HEAD, (head + 1) * HEAD)
        values_at = slice(COLS + head * HEAD, COLS + (head + 1) * HEAD)
        for block, out in ((left_ref, dleft_ref), (own_ref, down_ref), (right_ref, dright_ref)):
            unit_k, inv_k = unit(head_of(block, head).astype(F32))
            keys = unit_k.astype(BF16)
            probs = jnp.exp(SCALE * mul(query, keys, NT) + bias_ref[0, head]) * inverse
            grads = mul(grad, head_of(block, head, 1), NT)
            dscores = (probs * (grads - delta) * SCALE).astype(BF16)
            dquery += mul(dscores, keys, NN)
            out[:, keys_at] = unit_back(unit_k, inv_k, mul(dscores, query, TN)).astype(out.dtype)
            out[:, values_at] = mul(probs.astype(BF16), grad, TN).astype(out.dtype)
        weights, unit_v, inv_v = virtual_weights(bias_ref, head, unit_q, virtual_ref, member_ref)
        probs = weights * inverse
        wide = grad.astype(F32)
        grads = mul(wide, head_of(virtual_ref, head, 1), NT, PRECISE)
        dscores = probs * (grads - delta) * SCALE
        dquery += mul(dscores, unit_v, NN, PRECISE)
        dvirtual_ref[:, keys_at] = unit_back(unit_v, inv_v, mul(dscores, unit_q, TN, PRECISE))
        dvirtual_ref[:, values_at] = mul(probs, wide, TN, PRECISE)
        dquery_ref[:, keys_at] = unit_back(unit_q, inv_q, dquery).astype(BF16)


def total_kernel(asked_ref, back_ref, dquery_ref, down_ref, from_left_ref, from_right_ref, tail_ref, out_ref, work_ref):
    place = lax.broadcasted_iota(jnp.int32, (ROWS, SHARDS), 0)
    open_slots(work_ref, back_ref)
    rim = from_left_ref[...].astype(F32) + from_right_ref[...].astype(F32)
    hits = jnp.concatenate([ones_where(place == asked_ref[perm : perm + 1, :]) for perm in range(DEGREE)], axis=1)
    rows = jnp.concatenate([take_slots(work_ref, perm) for perm in range(DEGREE)], axis=0)
    total = down_ref[...] + rim + mul(hits, rows, NN)
    out_ref[:ROWS, :COLS] = dquery_ref[...]
    out_ref[:ROWS, COLS:] = total.astype(BF16)
    out_ref[ROWS:, :] = tail_ref[...]


def weight_kernel(in_own_ref, in_other_ref, own_ref, other_ref, out_ref):
    own, other = own_ref[...], other_ref[...]
    vnode = own[ROWS + 16 :].astype(F32) + other[ROWS + 16 :].astype(F32)
    high, low = two_terms(vnode[:8] + vnode[8:])
    tail = jnp.concatenate([high.astype(F32), low.astype(F32)], axis=0).astype(BF16)
    for part in range(4):
        at = slice(part * 128, (part + 1) * 128)
        term = mul(in_own_ref[at, :], own, NN) + mul(in_other_ref[at, :], other, NN)
        out_ref[part, :128, :] = term.astype(BF16)
        out_ref[part, 128:, :] = tail


def finish_kernel(parts_ref, weight_ref, vnode_ref):
    out_scale = 1.0 / math.sqrt(ROWS * SHARDS)
    total = parts_ref[0].astype(F32)
    for part in range(1, SIZES["z"]):
        total += parts_ref[part].astype(F32)
    total *= out_scale
    for kind in range(3):
        weight_ref[kind] = total[:, kind * COLS : (kind + 1) * COLS]
    vnode_ref[:, :512] = total[:VIRTUAL, 3 * COLS :]
    vnode_ref[:, 512:] = total[VIRTUAL:, 3 * COLS :]


VMEM = pl.BlockSpec(memory_space=pltpu.VMEM)
SMEM = pl.BlockSpec(memory_space=pltpu.SMEM)
WORK = (pltpu.VMEM((2, SHARDS * SLOTS, HEAD), F32),)


def call(kernel, outs, *args, scalars=0, scratch=(), flops=10**8):
    shapes = [jax.ShapeDtypeStruct(shape, kind) for shape, kind in outs]
    moved = sum(math.prod(a.shape) * a.dtype.itemsize for a in [*args, *shapes])
    return pl.pallas_call(
        kernel,
        out_shape=shapes,
        in_specs=[SMEM] * scalars + [VMEM] * (len(args) - scalars),
        out_specs=[VMEM] * len(shapes),
        scratch_shapes=list(scratch),
        compiler_params=pltpu.CompilerParams(vmem_limit_bytes=32 * 2**20),
        cost_estimate=pl.CostEstimate(flops=flops, bytes_accessed=moved, transcendentals=0),
    )(*args)


def exchange(values, axis):
    return lax.all_to_all(values, axis, split_axis=0, concat_axis=0, tiled=True)


def shift(values, axis, step):
    count = math.prod(SIZES[name] for name in axis) if isinstance(axis, tuple) else SIZES[axis]
    return lax.ppermute(values, axis, [(i, (i + step) % count) for i in range(count)])


def swap(values, axis, bit):
    return lax.ppermute(values, axis, [(i, i ^ bit) for i in range(SIZES[axis])])


def sum_of_four(values, axis):
    near, far, both = (swap(values, axis, bit) for bit in (1, 2, 3))
    return (values + near) + (far + both)


def two_terms(values):
    high = values.astype(BF16)
    return high, (values - high.astype(F32)).astype(BF16)


def body(features, qkv_weight, vnode_emb, edge_bias, out_grad, neighbours, member, tile_list, tile_count):
    width_in = qkv_weight.shape[0]
    with jax.named_scope("ask"):
        wanted, = call(ask_kernel, [((SHARDS, 1, DEGREE), jnp.int32)], neighbours)
        asked = exchange(wanted, NODES)
    with jax.named_scope("project"):
        flat_weight = qkv_weight.reshape(width_in, 3 * COLS)
        projected = jnp.dot(features, flat_weight, preferred_element_type=F32)
        query = projected[:, :COLS]
        kv = projected[:, COLS:].astype(BF16)
        virtual_kv = jnp.dot(vnode_emb, flat_weight[:, COLS:], preferred_element_type=F32)
        from_left = shift(kv, NODES, 1)
        from_right = shift(kv, NODES, -1)
    with jax.named_scope("select"):
        core = lax.axis_index("c")
        place = jnp.arange(width_in, dtype=jnp.int32)
        half, rest = place // 512, place % 512
        source = (rest // 8 % 16) * 64 + (rest // 128) * 16 + (half ^ core) * 8 + rest % 8
        chosen = (source[:, None] == jnp.arange(width_in, dtype=jnp.int32)[None, :]).astype(BF16)
        rows_in = jnp.concatenate([features, vnode_emb, vnode_emb, jnp.zeros((24, width_in), BF16)], axis=0)
        sorted_in = mul(chosen, rows_in, NT).astype(BF16)
        in_own = sorted_in[:512]
        in_other = jnp.concatenate([swap(sorted_in[512:, :ROWS], "c", 1), in_own[:, ROWS:]], axis=1)
        from_left, from_right, in_own, in_other = lax.optimization_barrier((from_left, from_right, in_own, in_other))
    with jax.named_scope("serve"):
        served, = call(serve_kernel, [((SHARDS * SLOTS, COLS), BF16)], asked, kv, scratch=WORK)
        near = exchange(served.reshape(SHARDS, SLOTS, COLS), NODES).reshape(SHARDS * SLOTS, COLS)
    with jax.named_scope("local"):
        sums, query_turned, grad_turned = call(
            local_kernel, [((2 * HEADS_DEV, ROWS), F32), ((COLS, ROWS), F32), ((COLS, ROWS), F32)],
            edge_bias, query, from_left, kv, from_right, out_grad, virtual_kv, member, scalars=1,
        )
    with jax.named_scope("near"):
        send, stats, dnear = call(
            near_kernel, [((SHARDS * SLOTS, COLS), BF16), ((2 * HEADS_DEV, ROWS), F32), ((COLS, ROWS), F32)],
            edge_bias, neighbours, query_turned, near, grad_turned, sums, scalars=1, scratch=WORK,
        )
        back = exchange(send.reshape(SHARDS, SLOTS, COLS), NODES).reshape(SHARDS * SLOTS, COLS)
    with jax.named_scope("back"):
        dquery, dleft, down, dright, dvirtual = call(
            back_kernel,
            [((ROWS, COLS), BF16), ((ROWS, 2 * COLS), BF16), ((ROWS, 2 * COLS), F32), ((ROWS, 2 * COLS), BF16), ((VIRTUAL, 2 * COLS), F32)],
            edge_bias, query, from_left, kv, from_right, out_grad, virtual_kv, member, stats, dnear, scalars=1,
        )
        back_left = shift(dright, NODES, 1)
        back_right = shift(dleft, NODES, -1)
    with jax.named_scope("virtual"):
        split = jnp.concatenate(two_terms(dvirtual), axis=0)
        vnode = mul(split, flat_weight[:, COLS:], NT)
        vnode = vnode[:VIRTUAL] + vnode[VIRTUAL:]
        vnode = sum_of_four(vnode, "mp")
        vnode = jnp.concatenate(two_terms(jnp.concatenate([vnode[:, :512], vnode[:, 512:]], axis=0)), axis=0)
        tail = jnp.concatenate([jnp.pad(split, ((0, 8), (COLS, 0))), jnp.pad(vnode, ((0, 0), (0, COLS)))], axis=0)
    with jax.named_scope("total"):
        own, = call(
            total_kernel, [((ROWS + 32, 3 * COLS), BF16)],
            asked.reshape(SHARDS, DEGREE).T, back, dquery, down, back_left, back_right, tail, scratch=WORK,
        )
        other = swap(own, "c", 1)
    with jax.named_scope("feature"):
        partial = mul(own[:ROWS], flat_weight, NT).astype(BF16)
        me = lax.axis_index("mp")
        summed = lax.dynamic_slice_in_dim(partial, me * COLS, COLS, 1).astype(F32)
        for step in range(1, 4):
            piece = lax.dynamic_slice_in_dim(partial, ((me + step) % 4) * COLS, COLS, 1)
            summed = summed + shift(piece, "mp", step).astype(F32)
        feature_grad = summed.astype(BF16)
    with jax.named_scope("weight"):
        term, = call(weight_kernel, [((4, 144, 3 * COLS), BF16)], in_own, in_other, own, other, flops=3 * 10**8)
        term = jnp.sum(exchange(term, "x").astype(F32), axis=0)
        vnode = term[128:136, :512] + term[136:, :512]
        tail = jnp.broadcast_to(vnode[None], (16, 8, 512))
        term = jnp.concatenate([term[:128].reshape(16, 8, 3 * COLS), tail], axis=2).astype(BF16)
        weight_grad, vnode_grad = call(
            finish_kernel, [((3, 8, COLS), F32), ((VIRTUAL, width_in), F32)], exchange(term, "z"),
        )
        weight_grad = weight_grad.transpose(1, 0, 2)
    return feature_grad, weight_grad, vnode_grad


def solution(mesh):
    fine = Mesh(mesh.devices.reshape(tuple(SIZES.values())), tuple(SIZES))
    return jax.shard_map(
        body,
        mesh=fine,
        in_specs=(
            P(NODES, None),
            P(None, None, "mp"),
            P(),
            P(None, "mp"),
            P(NODES, "mp"),
            P(None, NODES),
            P(NODES, None),
            P(NODES, None, None),
            P(NODES),
        ),
        out_specs=(P(NODES, "mp"), P(NODES, None, "mp"), P()),
        check_vma=False,
    )
```

```python
import math

import jax
import jax.numpy as jnp
from jax import lax
from jax.experimental import pallas as pl
from jax.experimental.pallas import tpu as pltpu
from jax.sharding import Mesh
from jax.sharding import PartitionSpec as P

HEAD = 128
TILE = 128
DEGREE = 4
VIRTUAL = 4
ROWS = 128
SHARDS = 128
COLS = 256
HEADS_DEV = 2
SLOTS = 2 * DEGREE
SIZES = {"z": 16, "x": 4, "c": 2, "mp": 4}
NODES = ("z", "x", "c")

SHARPNESS = 8.0
EPSILON = 1e-06
SCALE = SHARPNESS / HEAD
BOOST = math.log(TILE)
PRECISE = lax.Precision.HIGHEST
F32 = jnp.float32
BF16 = jnp.bfloat16

NN = (((1,), (0,)), ((), ()))
NT = (((1,), (1,)), ((), ()))
TN = (((0,), (0,)), ((), ()))


def mul(left, right, dims, precision=None):
    return lax.dot_general(left, right, dims, precision=precision, preferred_element_type=F32)


def unit(values):
    inv = lax.rsqrt(jnp.mean(values * values, axis=-1, keepdims=True) + EPSILON)
    return values * inv, inv


def unit_back(rows, inv, cotangent):
    return inv * (cotangent - rows * jnp.mean(rows * cotangent, axis=-1, keepdims=True))


def head_of(ref, head, part=0):
    start = part * COLS + head * HEAD
    return ref[:, start : start + HEAD]


def ones_where(condition):
    return jnp.where(condition, 1.0, 0.0).astype(BF16)


def shard_of(column):
    return lax.shift_right_logical(column, 7)


def ask_kernel(neighbours_ref, out_ref):
    shard = lax.broadcasted_iota(jnp.int32, (SHARDS, ROWS), 0)
    columns = []
    for perm in range(DEGREE):
        target = neighbours_ref[perm : perm + 1, :]
        rows = jnp.where(shard == shard_of(target), target & (ROWS - 1), 0)
        columns.append(jnp.sum(rows.astype(F32), axis=1, keepdims=True))
    out_ref[:, 0, :] = jnp.concatenate(columns, axis=1).astype(jnp.int32)


def slot(perm, part):
    return pl.ds(2 * perm + part, SHARDS, stride=SLOTS)


def take_slots(work_ref, perm):
    pieces = [work_ref[half, slot(perm, part), :] for part in range(2) for half in range(2)]
    return jnp.concatenate(pieces, axis=1).astype(BF16)


def put_slots(work_ref, perm, rows):
    for part in range(2):
        for half in range(2):
            at = part * COLS + half * HEAD
            work_ref[half, slot(perm, part), :] = rows[:, at : at + HEAD]


def open_slots(work_ref, rows_ref):
    for half in range(2):
        work_ref[half] = rows_ref[:, half * HEAD : (half + 1) * HEAD].astype(F32)


def close_slots(work_ref, rows_ref):
    for half in range(2):
        rows_ref[:, half * HEAD : (half + 1) * HEAD] = work_ref[half].astype(BF16)


def serve_kernel(asked_ref, kv_ref, out_ref, work_ref):
    row = lax.broadcasted_iota(jnp.int32, (SHARDS, ROWS), 1)
    asked = asked_ref[:, 0, :]
    hits = jnp.concatenate([ones_where(row == asked[:, perm : perm + 1]) for perm in range(DEGREE)], axis=0)
    picked = mul(hits, kv_ref[...], NN)
    for perm in range(DEGREE):
        put_slots(work_ref, perm, picked[perm * SHARDS : (perm + 1) * SHARDS])
    close_slots(work_ref, out_ref)


def virtual_weights(bias_ref, head, unit_q, virtual_ref, member_ref):
    unit_v, inv_v = unit(head_of(virtual_ref, head))
    scores = SCALE * mul(unit_q, unit_v, NT, PRECISE) + bias_ref[2, head] + BOOST
    return jnp.exp(scores) * member_ref[...].astype(F32), unit_v, inv_v


def turned(columns):
    wide = jnp.concatenate(columns + [jnp.zeros((ROWS, HEAD - len(columns)), F32)], axis=1)
    return wide.T[: len(columns)]


def local_kernel(bias_ref, query_ref, left_ref, own_ref, right_ref, grad_ref, virtual_ref, member_ref, sums_ref, query_out_ref, grad_out_ref):
    columns = []
    for head in range(HEADS_DEV):
        unit_q, _ = unit(head_of(query_ref, head))
        query = unit_q.astype(BF16)
        grad = head_of(grad_ref, head)
        total = jnp.zeros((ROWS, 1), F32)
        mixed = jnp.zeros((ROWS, 1), F32)
        for block in (left_ref, own_ref, right_ref):
            unit_k, _ = unit(head_of(block, head).astype(F32))
            weights = jnp.exp(SCALE * mul(query, unit_k.astype(BF16), NT) + bias_ref[0, head])
            grads = mul(grad, head_of(block, head, 1), NT)
            total += jnp.sum(weights, axis=1, keepdims=True)
            mixed += jnp.sum(weights * grads, axis=1, keepdims=True)
        weights, _, _ = virtual_weights(bias_ref, head, unit_q, virtual_ref, member_ref)
        grads = mul(grad.astype(F32), head_of(virtual_ref, head, 1), NT, PRECISE)
        total += jnp.sum(weights, axis=1, keepdims=True)
        mixed += jnp.sum(weights * grads, axis=1, keepdims=True)
        columns += [total, mixed]
        at = slice(head * HEAD, (head + 1) * HEAD)
        query_out_ref[at, :] = unit_q.T
        grad_out_ref[at, :] = grad.astype(F32).T
    sums_ref[...] = turned(columns)


def near_kernel(bias_ref, neighbours_ref, query_ref, near_ref, grad_ref, sums_ref, send_ref, stats_ref, dquery_ref, work_ref):
    totals = [sums_ref[2 * head : 2 * head + 1, :] for head in range(HEADS_DEV)]
    mixed = [sums_ref[2 * head + 1 : 2 * head + 2, :] for head in range(HEADS_DEV)]
    shard = lax.broadcasted_iota(jnp.int32, (SHARDS, ROWS), 0)
    hits = [ones_where(shard == shard_of(neighbours_ref[perm : perm + 1, :])) for perm in range(DEGREE)]
    unit_q = [query_ref[head * HEAD : (head + 1) * HEAD, :] for head in range(HEADS_DEV)]
    grad = [grad_ref[head * HEAD : (head + 1) * HEAD, :] for head in range(HEADS_DEV)]
    open_slots(work_ref, near_ref)
    saved = {}
    for perm in range(DEGREE):
        rows = mul(take_slots(work_ref, perm), hits[perm], TN)
        for head in range(HEADS_DEV):
            keys = rows[head * HEAD : (head + 1) * HEAD]
            values = rows[COLS + head * HEAD : COLS + (head + 1) * HEAD]
            inv_k = lax.rsqrt(jnp.mean(keys * keys, axis=0, keepdims=True) + EPSILON)
            unit_k = keys * inv_k
            product = jnp.sum(unit_q[head] * unit_k, axis=0, keepdims=True)
            weights = jnp.exp(SCALE * product + bias_ref[1, head] + BOOST)
            grads = jnp.sum(grad[head] * values, axis=0, keepdims=True)
            totals[head] = totals[head] + weights
            mixed[head] = mixed[head] + weights * grads
            saved[perm, head] = (unit_k, inv_k, product, weights, grads)
    inverse = [1.0 / total for total in totals]
    delta = [mixed[head] * inverse[head] for head in range(HEADS_DEV)]
    dquery = [jnp.zeros((HEAD, ROWS), F32) for _ in range(HEADS_DEV)]
    for perm in range(DEGREE):
        dkeys, dvalues = [], []
        for head in range(HEADS_DEV):
            unit_k, inv_k, product, weights, grads = saved[perm, head]
            probs = weights * inverse[head]
            dscores = probs * (grads - delta[head]) * SCALE
            dquery[head] = dquery[head] + dscores * unit_k
            factor = dscores * inv_k
            dkeys.append((factor * unit_q[head] - (factor * product * (1.0 / HEAD)) * unit_k).astype(BF16))
            dvalues.append((probs * grad[head]).astype(BF16))
        put_slots(work_ref, perm, mul(hits[perm], jnp.concatenate(dkeys + dvalues, axis=0), NT))
    close_slots(work_ref, send_ref)
    stats_ref[...] = jnp.concatenate([inverse[0], delta[0], inverse[1], delta[1]], axis=0)
    dquery_ref[...] = jnp.concatenate(dquery, axis=0)


def back_kernel(
    bias_ref, query_ref, left_ref, own_ref, right_ref, grad_ref, virtual_ref, member_ref, stats_ref, dnear_ref,
    dquery_ref, dleft_ref, down_ref, dright_ref, dvirtual_ref,
):
    stats = jnp.concatenate([stats_ref[...], jnp.zeros((HEAD - 2 * HEADS_DEV, ROWS), F32)], axis=0).T
    for head in range(HEADS_DEV):
        unit_q, inv_q = unit(head_of(query_ref, head))
        query = unit_q.astype(BF16)
        grad = head_of(grad_ref, head)
        inverse = stats[:, 2 * head : 2 * head + 1]
        delta = stats[:, 2 * head + 1 : 2 * head + 2]
        dquery = dnear_ref[head * HEAD : (head + 1) * HEAD, :].T
        keys_at = slice(head * HEAD, (head + 1) * HEAD)
        values_at = slice(COLS + head * HEAD, COLS + (head + 1) * HEAD)
        for block, out in ((left_ref, dleft_ref), (own_ref, down_ref), (right_ref, dright_ref)):
            unit_k, inv_k = unit(head_of(block, head).astype(F32))
            keys = unit_k.astype(BF16)
            probs = jnp.exp(SCALE * mul(query, keys, NT) + bias_ref[0, head]) * inverse
            grads = mul(grad, head_of(block, head, 1), NT)
            dscores = (probs * (grads - delta) * SCALE).astype(BF16)
            dquery += mul(dscores, keys, NN)
            out[:, keys_at] = unit_back(unit_k, inv_k, mul(dscores, query, TN)).astype(out.dtype)
            out[:, values_at] = mul(probs.astype(BF16), grad, TN).astype(out.dtype)
        weights, unit_v, inv_v = virtual_weights(bias_ref, head, unit_q, virtual_ref, member_ref)
        probs = weights * inverse
        wide = grad.astype(F32)
        grads = mul(wide, head_of(virtual_ref, head, 1), NT, PRECISE)
        dscores = probs * (grads - delta) * SCALE
        dquery += mul(dscores, unit_v, NN, PRECISE)
        dvirtual_ref[:, keys_at] = unit_back(unit_v, inv_v, mul(dscores, unit_q, TN, PRECISE))
        dvirtual_ref[:, values_at] = mul(probs, wide, TN, PRECISE)
        dquery_ref[:, keys_at] = unit_back(unit_q, inv_q, dquery).astype(BF16)


def total_kernel(asked_ref, back_ref, dquery_ref, down_ref, from_left_ref, from_right_ref, tail_ref, out_ref, work_ref):
    place = lax.broadcasted_iota(jnp.int32, (ROWS, SHARDS), 0)
    open_slots(work_ref, back_ref)
    rim = from_left_ref[...].astype(F32) + from_right_ref[...].astype(F32)
    hits = jnp.concatenate([ones_where(place == asked_ref[perm : perm + 1, :]) for perm in range(DEGREE)], axis=1)
    rows = jnp.concatenate([take_slots(work_ref, perm) for perm in range(DEGREE)], axis=0)
    total = down_ref[...] + rim + mul(hits, rows, NN)
    out_ref[:ROWS, :COLS] = dquery_ref[...]
    out_ref[:ROWS, COLS:] = total.astype(BF16)
    out_ref[ROWS:, :] = tail_ref[...]


def weight_kernel(in_own_ref, in_other_ref, own_ref, other_ref, out_ref):
    own, other = own_ref[...], other_ref[...]
    vnode = own[ROWS + 16 :].astype(F32) + other[ROWS + 16 :].astype(F32)
    vnode = vnode[:8] + vnode[8:]
    for part in range(4):
        at = slice(part * 128, (part + 1) * 128)
        term = mul(in_own_ref[at, :], own, NN) + mul(in_other_ref[at, :], other, NN)
        out_ref[part] = jnp.concatenate([term, vnode], axis=0).astype(BF16)


def finish_kernel(parts_ref, weight_ref, vnode_ref):
    out_scale = 1.0 / math.sqrt(ROWS * SHARDS)
    total = parts_ref[0].astype(F32)
    for part in range(1, SIZES["z"]):
        total += parts_ref[part].astype(F32)
    total *= out_scale
    for kind in range(3):
        weight_ref[kind] = total[:, kind * COLS : (kind + 1) * COLS]
    vnode_ref[:, :512] = total[:VIRTUAL, 3 * COLS :]
    vnode_ref[:, 512:] = total[VIRTUAL:, 3 * COLS :]


VMEM = pl.BlockSpec(memory_space=pltpu.VMEM)
SMEM = pl.BlockSpec(memory_space=pltpu.SMEM)
WORK = (pltpu.VMEM((2, SHARDS * SLOTS, HEAD), F32),)


def call(kernel, outs, *args, scalars=0, scratch=(), flops=10**8):
    shapes = [jax.ShapeDtypeStruct(shape, kind) for shape, kind in outs]
    moved = sum(math.prod(a.shape) * a.dtype.itemsize for a in [*args, *shapes])
    return pl.pallas_call(
        kernel,
        out_shape=shapes,
        in_specs=[SMEM] * scalars + [VMEM] * (len(args) - scalars),
        out_specs=[VMEM] * len(shapes),
        scratch_shapes=list(scratch),
        compiler_params=pltpu.CompilerParams(vmem_limit_bytes=32 * 2**20),
        cost_estimate=pl.CostEstimate(flops=flops, bytes_accessed=moved, transcendentals=0),
    )(*args)


def exchange(values, axis):
    return lax.all_to_all(values, axis, split_axis=0, concat_axis=0, tiled=True)


def shift(values, axis, step):
    count = math.prod(SIZES[name] for name in axis) if isinstance(axis, tuple) else SIZES[axis]
    return lax.ppermute(values, axis, [(i, (i + step) % count) for i in range(count)])


def swap(values, axis, bit):
    return lax.ppermute(values, axis, [(i, i ^ bit) for i in range(SIZES[axis])])


def sum_of_four(values, axis):
    near, far, both = (swap(values, axis, bit) for bit in (1, 2, 3))
    return (values + near) + (far + both)


def two_terms(values):
    high = values.astype(BF16)
    return high, (values - high.astype(F32)).astype(BF16)


def body(features, qkv_weight, vnode_emb, edge_bias, out_grad, neighbours, member, tile_list, tile_count):
    width_in = qkv_weight.shape[0]
    with jax.named_scope("ask"):
        wanted, = call(ask_kernel, [((SHARDS, 1, DEGREE), jnp.int32)], neighbours)
        asked = exchange(wanted, NODES)
    with jax.named_scope("project"):
        flat_weight = qkv_weight.reshape(width_in, 3 * COLS)
        projected = jnp.dot(features, flat_weight, preferred_element_type=F32)
        query = projected[:, :COLS]
        kv = projected[:, COLS:].astype(BF16)
        virtual_kv = jnp.dot(vnode_emb, flat_weight[:, COLS:], preferred_element_type=F32)
        from_left = shift(kv, NODES, 1)
        from_right = shift(kv, NODES, -1)
    with jax.named_scope("select"):
        core = lax.axis_index("c")
        place = jnp.arange(width_in, dtype=jnp.int32)
        half, rest = place // 512, place % 512
        source = (rest // 8 % 16) * 64 + (rest // 128) * 16 + (half ^ core) * 8 + rest % 8
        chosen = (source[:, None] == jnp.arange(width_in, dtype=jnp.int32)[None, :]).astype(BF16)
        rows_in = jnp.concatenate([features, vnode_emb, vnode_emb, jnp.zeros((24, width_in), BF16)], axis=0)
        sorted_in = mul(chosen, rows_in, NT).astype(BF16)
        in_own = sorted_in[:512]
        in_other = jnp.concatenate([swap(sorted_in[512:, :ROWS], "c", 1), in_own[:, ROWS:]], axis=1)
        from_left, from_right, in_own, in_other = lax.optimization_barrier((from_left, from_right, in_own, in_other))
    with jax.named_scope("serve"):
        served, = call(serve_kernel, [((SHARDS * SLOTS, COLS), BF16)], asked, kv, scratch=WORK)
        near = exchange(served.reshape(SHARDS, SLOTS, COLS), NODES).reshape(SHARDS * SLOTS, COLS)
    with jax.named_scope("local"):
        sums, query_turned, grad_turned = call(
            local_kernel, [((2 * HEADS_DEV, ROWS), F32), ((COLS, ROWS), F32), ((COLS, ROWS), F32)],
            edge_bias, query, from_left, kv, from_right, out_grad, virtual_kv, member, scalars=1,
        )
    with jax.named_scope("near"):
        send, stats, dnear = call(
            near_kernel, [((SHARDS * SLOTS, COLS), BF16), ((2 * HEADS_DEV, ROWS), F32), ((COLS, ROWS), F32)],
            edge_bias, neighbours, query_turned, near, grad_turned, sums, scalars=1, scratch=WORK,
        )
        back = exchange(send.reshape(SHARDS, SLOTS, COLS), NODES).reshape(SHARDS * SLOTS, COLS)
    with jax.named_scope("back"):
        dquery, dleft, down, dright, dvirtual = call(
            back_kernel,
            [((ROWS, COLS), BF16), ((ROWS, 2 * COLS), BF16), ((ROWS, 2 * COLS), F32), ((ROWS, 2 * COLS), BF16), ((VIRTUAL, 2 * COLS), F32)],
            edge_bias, query, from_left, kv, from_right, out_grad, virtual_kv, member, stats, dnear, scalars=1,
        )
        back_left = shift(dright, NODES, 1)
        back_right = shift(dleft, NODES, -1)
    with jax.named_scope("virtual"):
        split = jnp.concatenate(two_terms(dvirtual), axis=0)
        vnode = mul(split, flat_weight[:, COLS:], NT)
        vnode = vnode[:VIRTUAL] + vnode[VIRTUAL:]
        vnode = sum_of_four(vnode, "mp")
        vnode = jnp.concatenate(two_terms(jnp.concatenate([vnode[:, :512], vnode[:, 512:]], axis=0)), axis=0)
        tail = jnp.concatenate([jnp.pad(split, ((0, 8), (COLS, 0))), jnp.pad(vnode, ((0, 0), (0, COLS)))], axis=0)
    with jax.named_scope("total"):
        own, = call(
            total_kernel, [((ROWS + 32, 3 * COLS), BF16)],
            asked.reshape(SHARDS, DEGREE).T, back, dquery, down, back_left, back_right, tail, scratch=WORK,
        )
        other = swap(own, "c", 1)
    with jax.named_scope("feature"):
        partial = mul(own[:ROWS], flat_weight, NT).astype(BF16)
        me = lax.axis_index("mp")
        summed = lax.dynamic_slice_in_dim(partial, me * COLS, COLS, 1).astype(F32)
        for step in range(1, 4):
            piece = lax.dynamic_slice_in_dim(partial, ((me + step) % 4) * COLS, COLS, 1)
            summed = summed + shift(piece, "mp", step).astype(F32)
        feature_grad = summed.astype(BF16)
    with jax.named_scope("weight"):
        term, = call(weight_kernel, [((4, 136, 3 * COLS), BF16)], in_own, in_other, own, other, flops=3 * 10**8)
        term = jnp.sum(exchange(term, "x").astype(F32), axis=0)
        vnode = term[128:, :512]
        tail = jnp.broadcast_to(vnode[None], (16, 8, 512))
        term = jnp.concatenate([term[:128].reshape(16, 8, 3 * COLS), tail], axis=2).astype(BF16)
        weight_grad, vnode_grad = call(
            finish_kernel, [((3, 8, COLS), F32), ((VIRTUAL, width_in), F32)], exchange(term, "z"),
        )
        weight_grad = weight_grad.transpose(1, 0, 2)
    return feature_grad, weight_grad, vnode_grad


def solution(mesh):
    fine = Mesh(mesh.devices.reshape(tuple(SIZES.values())), tuple(SIZES))
    return jax.shard_map(
        body,
        mesh=fine,
        in_specs=(
            P(NODES, None),
            P(None, None, "mp"),
            P(),
            P(None, "mp"),
            P(NODES, "mp"),
            P(None, NODES),
            P(NODES, None),
            P(NODES, None, None),
            P(NODES),
        ),
        out_specs=(P(NODES, "mp"), P(NODES, None, "mp"), P()),
        check_vma=False,
    )
```

```python
import math

import jax
import jax.numpy as jnp
from jax import lax
from jax.experimental import pallas as pl
from jax.experimental.pallas import tpu as pltpu
from jax.sharding import Mesh
from jax.sharding import PartitionSpec as P

HEAD = 128
TILE = 128
DEGREE = 4
VIRTUAL = 4
ROWS = 128
SHARDS = 128
COLS = 256
HEADS_DEV = 2
SLOTS = 2 * DEGREE
SIZES = {"z": 16, "x": 4, "c": 2, "mp": 4}
NODES = ("z", "x", "c")

SHARPNESS = 8.0
EPSILON = 1e-06
SCALE = SHARPNESS / HEAD
BOOST = math.log(TILE)
PRECISE = lax.Precision.HIGHEST
F32 = jnp.float32
BF16 = jnp.bfloat16

NN = (((1,), (0,)), ((), ()))
NT = (((1,), (1,)), ((), ()))
TN = (((0,), (0,)), ((), ()))


def mul(left, right, dims, precision=None):
    return lax.dot_general(left, right, dims, precision=precision, preferred_element_type=F32)


def unit(values):
    inv = lax.rsqrt(jnp.mean(values * values, axis=-1, keepdims=True) + EPSILON)
    return values * inv, inv


def unit_back(rows, inv, cotangent):
    return inv * (cotangent - rows * jnp.mean(rows * cotangent, axis=-1, keepdims=True))


def head_of(ref, head, part=0):
    start = part * COLS + head * HEAD
    return ref[:, start : start + HEAD]


def ones_where(condition):
    return jnp.where(condition, 1.0, 0.0).astype(BF16)


def shard_of(column):
    return lax.shift_right_logical(column, 7)


def ask_kernel(neighbours_ref, out_ref):
    shard = lax.broadcasted_iota(jnp.int32, (SHARDS, ROWS), 0)
    columns = []
    for perm in range(DEGREE):
        target = neighbours_ref[perm : perm + 1, :]
        rows = jnp.where(shard == shard_of(target), target & (ROWS - 1), 0)
        columns.append(jnp.sum(rows.astype(F32), axis=1, keepdims=True))
    out_ref[:, 0, :] = jnp.concatenate(columns, axis=1).astype(jnp.int32)


def slot(perm, part):
    return pl.ds(2 * perm + part, SHARDS, stride=SLOTS)


def take_slots(work_ref, perm):
    pieces = [work_ref[half, slot(perm, part), :] for part in range(2) for half in range(2)]
    return jnp.concatenate(pieces, axis=1).astype(BF16)


def put_slots(work_ref, perm, rows):
    for part in range(2):
        for half in range(2):
            at = part * COLS + half * HEAD
            work_ref[half, slot(perm, part), :] = rows[:, at : at + HEAD]


def open_slots(work_ref, rows_ref):
    for half in range(2):
        work_ref[half] = rows_ref[:, half * HEAD : (half + 1) * HEAD].astype(F32)


def close_slots(work_ref, rows_ref):
    for half in range(2):
        rows_ref[:, half * HEAD : (half + 1) * HEAD] = work_ref[half].astype(BF16)


def serve_kernel(asked_ref, kv_ref, out_ref, work_ref):
    row = lax.broadcasted_iota(jnp.int32, (SHARDS, ROWS), 1)
    asked = asked_ref[:, 0, :]
    hits = jnp.concatenate([ones_where(row == asked[:, perm : perm + 1]) for perm in range(DEGREE)], axis=0)
    picked = mul(hits, kv_ref[...], NN)
    for perm in range(DEGREE):
        put_slots(work_ref, perm, picked[perm * SHARDS : (perm + 1) * SHARDS])
    close_slots(work_ref, out_ref)


def virtual_weights(bias_ref, head, unit_q, virtual_ref, member_ref):
    unit_v, inv_v = unit(head_of(virtual_ref, head))
    scores = SCALE * mul(unit_q, unit_v, NT, PRECISE) + bias_ref[2, head] + BOOST
    return jnp.exp(scores) * member_ref[...].astype(F32), unit_v, inv_v


def turned(columns):
    wide = jnp.concatenate(columns + [jnp.zeros((ROWS, HEAD - len(columns)), F32)], axis=1)
    return wide.T[: len(columns)]


def local_kernel(bias_ref, query_ref, left_ref, own_ref, right_ref, grad_ref, virtual_ref, member_ref, sums_ref, query_out_ref, grad_out_ref):
    columns = []
    for head in range(HEADS_DEV):
        unit_q, _ = unit(head_of(query_ref, head))
        query = unit_q.astype(BF16)
        grad = head_of(grad_ref, head)
        total = jnp.zeros((ROWS, 1), F32)
        mixed = jnp.zeros((ROWS, 1), F32)
        for block in (left_ref, own_ref, right_ref):
            unit_k, _ = unit(head_of(block, head).astype(F32))
            weights = jnp.exp(SCALE * mul(query, unit_k.astype(BF16), NT) + bias_ref[0, head])
            grads = mul(grad, head_of(block, head, 1), NT)
            total += jnp.sum(weights, axis=1, keepdims=True)
            mixed += jnp.sum(weights * grads, axis=1, keepdims=True)
        weights, _, _ = virtual_weights(bias_ref, head, unit_q, virtual_ref, member_ref)
        grads = mul(grad.astype(F32), head_of(virtual_ref, head, 1), NT, PRECISE)
        total += jnp.sum(weights, axis=1, keepdims=True)
        mixed += jnp.sum(weights * grads, axis=1, keepdims=True)
        columns += [total, mixed]
        at = slice(head * HEAD, (head + 1) * HEAD)
        query_out_ref[at, :] = unit_q.T
        grad_out_ref[at, :] = grad.astype(F32).T
    sums_ref[...] = turned(columns)


def near_kernel(bias_ref, neighbours_ref, query_ref, near_ref, grad_ref, sums_ref, send_ref, stats_ref, dquery_ref, work_ref):
    totals = [sums_ref[2 * head : 2 * head + 1, :] for head in range(HEADS_DEV)]
    mixed = [sums_ref[2 * head + 1 : 2 * head + 2, :] for head in range(HEADS_DEV)]
    shard = lax.broadcasted_iota(jnp.int32, (SHARDS, ROWS), 0)
    hits = [ones_where(shard == shard_of(neighbours_ref[perm : perm + 1, :])) for perm in range(DEGREE)]
    unit_q = [query_ref[head * HEAD : (head + 1) * HEAD, :] for head in range(HEADS_DEV)]
    grad = [grad_ref[head * HEAD : (head + 1) * HEAD, :] for head in range(HEADS_DEV)]
    open_slots(work_ref, near_ref)
    saved = {}
    for perm in range(DEGREE):
        rows = mul(take_slots(work_ref, perm), hits[perm], TN)
        for head in range(HEADS_DEV):
            keys = rows[head * HEAD : (head + 1) * HEAD]
            values = rows[COLS + head * HEAD : COLS + (head + 1) * HEAD]
            inv_k = lax.rsqrt(jnp.mean(keys * keys, axis=0, keepdims=True) + EPSILON)
            unit_k = keys * inv_k
            product = jnp.sum(unit_q[head] * unit_k, axis=0, keepdims=True)
            weights = jnp.exp(SCALE * product + bias_ref[1, head] + BOOST)
            grads = jnp.sum(grad[head] * values, axis=0, keepdims=True)
            totals[head] = totals[head] + weights
            mixed[head] = mixed[head] + weights * grads
            saved[perm, head] = (unit_k, inv_k, product, weights, grads)
    inverse = [1.0 / total for total in totals]
    delta = [mixed[head] * inverse[head] for head in range(HEADS_DEV)]
    dquery = [jnp.zeros((HEAD, ROWS), F32) for _ in range(HEADS_DEV)]
    for perm in range(DEGREE):
        dkeys, dvalues = [], []
        for head in range(HEADS_DEV):
            unit_k, inv_k, product, weights, grads = saved[perm, head]
            probs = weights * inverse[head]
            dscores = probs * (grads - delta[head]) * SCALE
            dquery[head] = dquery[head] + dscores * unit_k
            factor = dscores * inv_k
            dkeys.append((factor * unit_q[head] - (factor * product * (1.0 / HEAD)) * unit_k).astype(BF16))
            dvalues.append((probs * grad[head]).astype(BF16))
        put_slots(work_ref, perm, mul(hits[perm], jnp.concatenate(dkeys + dvalues, axis=0), NT))
    close_slots(work_ref, send_ref)
    stats_ref[...] = jnp.concatenate([inverse[0], delta[0], inverse[1], delta[1]], axis=0)
    dquery_ref[...] = jnp.concatenate(dquery, axis=0)


def back_kernel(
    bias_ref, query_ref, left_ref, own_ref, right_ref, grad_ref, virtual_ref, member_ref, stats_ref, dnear_ref,
    dquery_ref, dleft_ref, down_ref, dright_ref, dvirtual_ref,
):
    stats = jnp.concatenate([stats_ref[...], jnp.zeros((HEAD - 2 * HEADS_DEV, ROWS), F32)], axis=0).T
    for head in range(HEADS_DEV):
        unit_q, inv_q = unit(head_of(query_ref, head))
        query = unit_q.astype(BF16)
        grad = head_of(grad_ref, head)
        inverse = stats[:, 2 * head : 2 * head + 1]
        delta = stats[:, 2 * head + 1 : 2 * head + 2]
        dquery = dnear_ref[head * HEAD : (head + 1) * HEAD, :].T
        keys_at = slice(head * HEAD, (head + 1) * HEAD)
        values_at = slice(COLS + head * HEAD, COLS + (head + 1) * HEAD)
        for block, out in ((left_ref, dleft_ref), (own_ref, down_ref), (right_ref, dright_ref)):
            unit_k, inv_k = unit(head_of(block, head).astype(F32))
            keys = unit_k.astype(BF16)
            probs = jnp.exp(SCALE * mul(query, keys, NT) + bias_ref[0, head]) * inverse
            grads = mul(grad, head_of(block, head, 1), NT)
            dscores = (probs * (grads - delta) * SCALE).astype(BF16)
            dquery += mul(dscores, keys, NN)
            out[:, keys_at] = unit_back(unit_k, inv_k, mul(dscores, query, TN)).astype(out.dtype)
            out[:, values_at] = mul(probs.astype(BF16), grad, TN).astype(out.dtype)
        weights, unit_v, inv_v = virtual_weights(bias_ref, head, unit_q, virtual_ref, member_ref)
        probs = weights * inverse
        wide = grad.astype(F32)
        grads = mul(wide, head_of(virtual_ref, head, 1), NT, PRECISE)
        dscores = probs * (grads - delta) * SCALE
        dquery += mul(dscores, unit_v, NN, PRECISE)
        dvirtual_ref[:, keys_at] = unit_back(unit_v, inv_v, mul(dscores, unit_q, TN, PRECISE))
        dvirtual_ref[:, values_at] = mul(probs, wide, TN, PRECISE)
        dquery_ref[:, keys_at] = unit_back(unit_q, inv_q, dquery).astype(BF16)


def total_kernel(asked_ref, back_ref, dquery_ref, down_ref, from_left_ref, from_right_ref, tail_ref, out_ref, work_ref):
    place = lax.broadcasted_iota(jnp.int32, (ROWS, SHARDS), 0)
    open_slots(work_ref, back_ref)
    rim = from_left_ref[...].astype(F32) + from_right_ref[...].astype(F32)
    hits = jnp.concatenate([ones_where(place == asked_ref[perm : perm + 1, :]) for perm in range(DEGREE)], axis=1)
    rows = jnp.concatenate([take_slots(work_ref, perm) for perm in range(DEGREE)], axis=0)
    total = down_ref[...] + rim + mul(hits, rows, NN)
    out_ref[:ROWS, :COLS] = dquery_ref[...]
    out_ref[:ROWS, COLS:] = total.astype(BF16)
    out_ref[ROWS:, :] = tail_ref[...]


def weight_kernel(in_own_ref, in_other_ref, own_ref, other_ref, out_ref):
    own, other = own_ref[...], other_ref[...]
    vnode = own[ROWS + 16 :].astype(F32) + other[ROWS + 16 :].astype(F32)
    vnode = vnode[:8] + vnode[8:]
    for part in range(4):
        at = slice(part * 128, (part + 1) * 128)
        term = mul(in_own_ref[at, :], own, NN) + mul(in_other_ref[at, :], other, NN)
        out_ref[part] = jnp.concatenate([term, vnode], axis=0).astype(BF16)


def spread_kernel(parts_ref, out_ref):
    total = parts_ref[0].astype(F32)
    for part in range(1, SIZES["x"]):
        total += parts_ref[part].astype(F32)
    for part in range(SIZES["z"]):
        rows = [total[part * 8 : (part + 1) * 8], total[128:, :512]]
        out_ref[part] = jnp.concatenate(rows, axis=1).astype(BF16)


def finish_kernel(parts_ref, weight_ref, vnode_ref):
    out_scale = 1.0 / math.sqrt(ROWS * SHARDS)
    total = parts_ref[0].astype(F32)
    for part in range(1, SIZES["z"]):
        total += parts_ref[part].astype(F32)
    total *= out_scale
    for kind in range(3):
        weight_ref[kind] = total[:, kind * COLS : (kind + 1) * COLS]
    vnode_ref[:, :512] = total[:VIRTUAL, 3 * COLS :]
    vnode_ref[:, 512:] = total[VIRTUAL:, 3 * COLS :]


VMEM = pl.BlockSpec(memory_space=pltpu.VMEM)
SMEM = pl.BlockSpec(memory_space=pltpu.SMEM)
WORK = (pltpu.VMEM((2, SHARDS * SLOTS, HEAD), F32),)


def call(kernel, outs, *args, scalars=0, scratch=(), flops=10**8):
    shapes = [jax.ShapeDtypeStruct(shape, kind) for shape, kind in outs]
    moved = sum(math.prod(a.shape) * a.dtype.itemsize for a in [*args, *shapes])
    return pl.pallas_call(
        kernel,
        out_shape=shapes,
        in_specs=[SMEM] * scalars + [VMEM] * (len(args) - scalars),
        out_specs=[VMEM] * len(shapes),
        scratch_shapes=list(scratch),
        compiler_params=pltpu.CompilerParams(vmem_limit_bytes=32 * 2**20),
        cost_estimate=pl.CostEstimate(flops=flops, bytes_accessed=moved, transcendentals=0),
    )(*args)


def exchange(values, axis):
    return lax.all_to_all(values, axis, split_axis=0, concat_axis=0, tiled=True)


def shift(values, axis, step):
    count = math.prod(SIZES[name] for name in axis) if isinstance(axis, tuple) else SIZES[axis]
    return lax.ppermute(values, axis, [(i, (i + step) % count) for i in range(count)])


def swap(values, axis, bit):
    return lax.ppermute(values, axis, [(i, i ^ bit) for i in range(SIZES[axis])])


def sum_of_four(values, axis):
    near, far, both = (swap(values, axis, bit) for bit in (1, 2, 3))
    return (values + near) + (far + both)


def two_terms(values):
    high = values.astype(BF16)
    return high, (values - high.astype(F32)).astype(BF16)


def body(features, qkv_weight, vnode_emb, edge_bias, out_grad, neighbours, member, tile_list, tile_count):
    width_in = qkv_weight.shape[0]
    with jax.named_scope("ask"):
        wanted, = call(ask_kernel, [((SHARDS, 1, DEGREE), jnp.int32)], neighbours)
        asked = exchange(wanted, NODES)
    with jax.named_scope("project"):
        flat_weight = qkv_weight.reshape(width_in, 3 * COLS)
        projected = jnp.dot(features, flat_weight, preferred_element_type=F32)
        query = projected[:, :COLS]
        kv = projected[:, COLS:].astype(BF16)
        virtual_kv = jnp.dot(vnode_emb, flat_weight[:, COLS:], preferred_element_type=F32)
        from_left = shift(kv, NODES, 1)
        from_right = shift(kv, NODES, -1)
    with jax.named_scope("select"):
        core = lax.axis_index("c")
        place = jnp.arange(width_in, dtype=jnp.int32)
        half, rest = place // 512, place % 512
        source = (rest // 8 % 16) * 64 + (rest // 128) * 16 + (half ^ core) * 8 + rest % 8
        chosen = (source[:, None] == jnp.arange(width_in, dtype=jnp.int32)[None, :]).astype(BF16)
        rows_in = jnp.concatenate([features, vnode_emb, vnode_emb, jnp.zeros((24, width_in), BF16)], axis=0)
        sorted_in = mul(chosen, rows_in, NT).astype(BF16)
        in_own = sorted_in[:512]
        in_other = jnp.concatenate([swap(sorted_in[512:, :ROWS], "c", 1), in_own[:, ROWS:]], axis=1)
        from_left, from_right, in_own, in_other = lax.optimization_barrier((from_left, from_right, in_own, in_other))
    with jax.named_scope("serve"):
        served, = call(serve_kernel, [((SHARDS * SLOTS, COLS), BF16)], asked, kv, scratch=WORK)
        near = exchange(served.reshape(SHARDS, SLOTS, COLS), NODES).reshape(SHARDS * SLOTS, COLS)
    with jax.named_scope("local"):
        sums, query_turned, grad_turned = call(
            local_kernel, [((2 * HEADS_DEV, ROWS), F32), ((COLS, ROWS), F32), ((COLS, ROWS), F32)],
            edge_bias, query, from_left, kv, from_right, out_grad, virtual_kv, member, scalars=1,
        )
    with jax.named_scope("near"):
        send, stats, dnear = call(
            near_kernel, [((SHARDS * SLOTS, COLS), BF16), ((2 * HEADS_DEV, ROWS), F32), ((COLS, ROWS), F32)],
            edge_bias, neighbours, query_turned, near, grad_turned, sums, scalars=1, scratch=WORK,
        )
        back = exchange(send.reshape(SHARDS, SLOTS, COLS), NODES).reshape(SHARDS * SLOTS, COLS)
    with jax.named_scope("back"):
        dquery, dleft, down, dright, dvirtual = call(
            back_kernel,
            [((ROWS, COLS), BF16), ((ROWS, 2 * COLS), BF16), ((ROWS, 2 * COLS), F32), ((ROWS, 2 * COLS), BF16), ((VIRTUAL, 2 * COLS), F32)],
            edge_bias, query, from_left, kv, from_right, out_grad, virtual_kv, member, stats, dnear, scalars=1,
        )
        back_left = shift(dright, NODES, 1)
        back_right = shift(dleft, NODES, -1)
    with jax.named_scope("virtual"):
        split = jnp.concatenate(two_terms(dvirtual), axis=0)
        vnode = mul(split, flat_weight[:, COLS:], NT)
        vnode = vnode[:VIRTUAL] + vnode[VIRTUAL:]
        vnode = sum_of_four(vnode, "mp")
        vnode = jnp.concatenate(two_terms(jnp.concatenate([vnode[:, :512], vnode[:, 512:]], axis=0)), axis=0)
        tail = jnp.concatenate([jnp.pad(split, ((0, 8), (COLS, 0))), jnp.pad(vnode, ((0, 0), (0, COLS)))], axis=0)
    with jax.named_scope("total"):
        own, = call(
            total_kernel, [((ROWS + 32, 3 * COLS), BF16)],
            asked.reshape(SHARDS, DEGREE).T, back, dquery, down, back_left, back_right, tail, scratch=WORK,
        )
        other = swap(own, "c", 1)
    with jax.named_scope("feature"):
        partial = mul(own[:ROWS], flat_weight, NT).astype(BF16)
        me = lax.axis_index("mp")
        summed = lax.dynamic_slice_in_dim(partial, me * COLS, COLS, 1).astype(F32)
        for step in range(1, 4):
            piece = lax.dynamic_slice_in_dim(partial, ((me + step) % 4) * COLS, COLS, 1)
            summed = summed + shift(piece, "mp", step).astype(F32)
        feature_grad = summed.astype(BF16)
    with jax.named_scope("weight"):
        term, = call(weight_kernel, [((4, 136, 3 * COLS), BF16)], in_own, in_other, own, other, flops=3 * 10**8)
        term, = call(spread_kernel, [((16, 8, 3 * COLS + 512), BF16)], exchange(term, "x"))
        weight_grad, vnode_grad = call(
            finish_kernel, [((3, 8, COLS), F32), ((VIRTUAL, width_in), F32)], exchange(term, "z"),
        )
        weight_grad = weight_grad.transpose(1, 0, 2)
    return feature_grad, weight_grad, vnode_grad


def solution(mesh):
    fine = Mesh(mesh.devices.reshape(tuple(SIZES.values())), tuple(SIZES))
    return jax.shard_map(
        body,
        mesh=fine,
        in_specs=(
            P(NODES, None),
            P(None, None, "mp"),
            P(),
            P(None, "mp"),
            P(NODES, "mp"),
            P(None, NODES),
            P(NODES, None),
            P(NODES, None, None),
            P(NODES),
        ),
        out_specs=(P(NODES, "mp"), P(NODES, None, "mp"), P()),
        check_vma=False,
    )
```
